256 devices in a mesh: mem: 64 (over y, z_hi, x, core), qry: 4 (over z_lo).
Axes of the slice: x: 4, y: 4, z: 8 (z_hi: 2, z_lo: 4; z = z_hi * 4 + z_lo), core: 2. Of those that a mesh axis runs over, the one named last changes fastest.
Arguments:
- queries: bfloat16 [1024, 4096], P('qry', 'mem'), may hold values from -6 to 6
- outputs: bfloat16 [1024, 4096], P('qry', 'mem'), may hold values from -6 to 6
- cotangent: bfloat16 [1024, 4096], P('qry', 'mem'), may hold values from -3072 to 3072
- log_norms: float32 [1024, 16], P('qry'), as said below
- memory_keys: bfloat16 [32768, 4096], P(('mem', 'qry')), may hold values from -6 to 6
- memory_values: bfloat16 [32768, 4096], P(('mem', 'qry')), may hold values from -6 to 6
Outputs:
- query_grads: bfloat16 [1024, 4096], P('qry', 'mem')
- key_grads: bfloat16 [32768, 4096], P(('mem', 'qry'))
- value_grads: bfloat16 [32768, 4096], P(('mem', 'qry'))
The draws below stay inside these ranges and needn't reach their ends.
Inputs may be any that keep to these rules, and one draw needn't show every extreme that they name: `log_norms`: each entry lies within half a unit of log(32768) + 0.5.
All inputs are finite; a program needn't handle non-finite values.
Results may differ from the reference program's by a relative error of at most 0.018.
Values may be sent and summed in bfloat16 or wider, within the bound.
No kernel may reach another device: no remote copies, remote signals or barrier semaphores. Data moves between devices by JAX's collectives and lax.ppermute only.
A program may use at most 128 MiB of HBM per device.

```python
import math
import jax
import jax.numpy as jnp
from jax import lax

H = 16
DH = 256
QRY_DEV = 256
MEM_DEV = 128
TARGETS = 1024
MEMORY = 32768
N_MEM = 64
N_QRY = 4


def draw_log_norms(key, part):
    key = jax.random.fold_in(key, 7)
    centre = math.log(MEMORY) + 0.5
    spread = jax.random.uniform(key, (TARGETS, H), jnp.float32, -0.5, 0.5)
    return centre + spread


def steps_of(rng, dims, shards, least, largest):
    def one(axis_at, blocks):
        heights = jax.random.uniform(jax.random.fold_in(jax.random.fold_in(rng, 6), axis_at), (blocks,), jnp.float32, least / len(shards), largest / len(shards))
        return jnp.repeat(jnp.exp(heights), dims[axis_at] // blocks).reshape((-1,) + (1,) * (len(dims) - axis_at - 1))

    loudness = one(*shards[0])
    for cut in shards[1:]:
        loudness = loudness * one(*cut)
    return loudness


def noise(stream_key, dims, deviation, reach, split=(), kind=jnp.bfloat16):
    factor_of = steps_of(stream_key, dims, split, -0.22, 0.18) if split else 1.0
    result = jax.random.normal(stream_key, dims, jnp.float32) * deviation * factor_of
    return jnp.minimum(jnp.maximum(result, -reach), reach).astype(kind)


def setup_inputs(seed: int = 0) -> dict:
    keys = jax.random.split(jax.random.key(seed), 7)
    queries = noise(keys[0], (TARGETS, H * DH), 1.0, 6.0, ((0, 4), (1, 64)))
    outputs = noise(keys[1], (TARGETS, H * DH), 1.0, 6.0, ((0, 4), (1, 64)))
    cotangent = noise(keys[2], (TARGETS, H * DH), (MEMORY // 64), 3072.0, ((0, 4), (1, 64)))
    log_norms = draw_log_norms(jax.random.fold_in(keys[6], 71), 0)
    memory_keys = noise(keys[4], (MEMORY, H * DH), 1.0, 6.0, ((0, 256),))
    memory_values = noise(keys[5], (MEMORY, H * DH), 1.0, 6.0, ((0, 256),))
    return {"queries": queries, "outputs": outputs, "cotangent": cotangent, "log_norms": log_norms, "memory_keys": memory_keys, "memory_values": memory_values}


def rounded(values):
    return lax.optimization_barrier(values.astype(jnp.bfloat16)).astype(jnp.float32)


def reference(queries, outputs, cotangent, log_norms, memory_keys, memory_values):
    target_rows, model_width = queries.shape
    head_count = log_norms.shape[1]
    head_width = model_width // head_count
    factor = head_width ** -0.5
    highest = lax.Precision.HIGHEST
    query_heads = queries.astype(jnp.float32).reshape(target_rows, head_count, head_width)
    cotangent_heads = cotangent.astype(jnp.float32).reshape(target_rows, head_count, head_width)
    output_heads = outputs.astype(jnp.float32).reshape(target_rows, head_count, head_width)
    row_sums = jnp.sum(cotangent_heads * output_heads, axis=2)
    offsets = jnp.transpose(log_norms)[:, :, None]
    centres = jnp.transpose(row_sums)[:, :, None]
    group_rows = MEM_DEV * N_QRY
    key_blocks = memory_keys.reshape(N_MEM, group_rows, head_count, head_width)
    value_blocks = memory_values.reshape(N_MEM, group_rows, head_count, head_width)
    query_shards = query_heads.reshape(N_QRY, QRY_DEV, head_count, head_width)
    cotangent_shards = cotangent_heads.reshape(N_QRY, QRY_DEV, head_count, head_width)

    def advance(running, blocks):
        key_block = blocks[0].astype(jnp.float32)
        value_block = blocks[1].astype(jnp.float32)
        scores = jnp.einsum("qhd,khd->hqk", query_heads, key_block, precision=highest) * factor
        weights = jnp.exp(scores - offsets)
        slopes = jnp.einsum("qhd,khd->hqk", cotangent_heads, value_block, precision=highest)
        score_grads = rounded(weights * (slopes - centres))
        weights_low = rounded(weights)
        running = running + jnp.einsum("hqk,khd->qhd", score_grads, key_block, precision=highest) * factor
        grads_split = score_grads.reshape(head_count, N_QRY, QRY_DEV, group_rows)
        weights_split = weights_low.reshape(head_count, N_QRY, QRY_DEV, group_rows)
        key_parts = jnp.einsum("hnqk,nqhd->nkhd", grads_split, query_shards, precision=highest) * factor
        value_parts = jnp.einsum("hnqk,nqhd->nkhd", weights_split, cotangent_shards, precision=highest)
        key_total = jnp.sum(rounded(key_parts), axis=0).astype(jnp.bfloat16)
        value_total = jnp.sum(rounded(value_parts), axis=0).astype(jnp.bfloat16)
        return running, (key_total, value_total)

    initial = jnp.zeros((target_rows, head_count, head_width), jnp.float32)
    running, (key_totals, value_totals) = lax.scan(advance, initial, (key_blocks, value_blocks))
    query_grads = running.reshape(target_rows, model_width).astype(jnp.bfloat16)
    key_grads = key_totals.reshape(-1, model_width)
    value_grads = value_totals.reshape(-1, model_width)
    return (query_grads, key_grads, value_grads)
```

```python
import jax
import jax.numpy as jnp
from jax import lax
from jax.experimental import pallas as pl
from jax.experimental.pallas import tpu as pltpu
from jax.sharding import Mesh, PartitionSpec as P

AXES = ("y", "zh", "x", "core", "zl")
SIZES = (4, 2, 4, 2, 4)
MEM = ("y", "zh", "x", "core")
PLANE_Z = ("zh", "zl")
HEADS = 16
DH = 256
ROWS = 256
PART = 64
KEYS = 128
STAT = 16
MESSAGE = 2 * PART + STAT
FACTOR = DH**-0.5
LOG2E = 1.4426950408889634
SLOTS = [(dy, dc) for dy in (0, 1, 2, 3) for dc in (0, 1)]
BF16, F32 = jnp.bfloat16, jnp.float32
ANY = pl.BlockSpec(memory_space=pl.ANY)
VMEM = pl.BlockSpec(memory_space=pltpu.VMEM)


def memory_pairs(dy, dc):
    return [
        (y * 2 + c, ((y + dy) % 4) * 2 + (c ^ dc)) for y in range(4) for c in range(2)
    ]


def plane_pairs(k):
    return [
        ((2 * xh + j // 2) * 2 + j % 2, (j ^ k) * 2 + xh)
        for xh in range(2)
        for j in range(4)
    ]


def inverse(pairs):
    return [(b, a) for a, b in pairs]


def pieces(value):
    high = value.astype(BF16)
    rest = value - high.astype(F32)
    middle = rest.astype(BF16)
    low = (rest - middle.astype(F32)).astype(BF16)
    return [high, middle, low]


def message_kernel(queries, outputs, cotangent, log_norms, message):
    sums = jnp.sum(
        cotangent[...].astype(F32) * outputs[...].astype(F32), axis=0, keepdims=True
    )
    zh, x, y = lax.axis_index("zh"), lax.axis_index("x"), lax.axis_index("y")
    head = 4 * y + 2 * zh + x // 2
    mine = lax.broadcasted_iota(jnp.int32, (HEADS, ROWS), 0) == head
    norms = jnp.sum(jnp.where(mine, log_norms[...], 0.0), axis=0, keepdims=True)
    rows = [r.astype(F32) for r in pieces(sums) + pieces(norms)]
    stat = jnp.concatenate(rows + [jnp.zeros((STAT - 6, ROWS), F32)], axis=0).astype(BF16)
    for z in range(8):
        message[z, :PART, :] = queries[...]
        message[z, PART : 2 * PART, :] = cotangent[...]
        message[z, 2 * PART :, :] = stat


def make_message(queries, outputs, cotangent, log_norms):
    return pl.pallas_call(
        message_kernel,
        out_shape=jax.ShapeDtypeStruct((8, MESSAGE, ROWS), BF16),
        in_specs=[VMEM] * 4,
        out_specs=VMEM,
        name="message",
    )(queries, outputs, cotangent, log_norms)


def slot_columns(dy, dc, zh):
    y, core = lax.axis_index("y"), lax.axis_index("core")
    owner = lax.rem(y + dy, 4)
    half = core if dc == 0 else 1 - core
    return pl.ds(pl.multiple_of((4 * owner + 2 * zh + half) * DH, DH), DH)


def split_kernel(keys, values, *refs):
    outs, sem = refs[:8], refs[8]
    copies = []
    for s, (dy, dc) in enumerate(SLOTS):
        for zh in range(2):
            for a, array in enumerate((keys, values)):
                copies.append(
                    pltpu.make_async_copy(
                        array.at[:, slot_columns(dy, dc, zh)],
                        outs[s].at[a, zh],
                        sem.at[len(copies)],
                    )
                )
    for copy in copies:
        copy.start()
    for copy in copies:
        copy.wait()


def split(keys, values):
    return pl.pallas_call(
        split_kernel,
        out_shape=[jax.ShapeDtypeStruct((2, 2, KEYS, DH), BF16)] * 8,
        in_specs=[ANY] * 2,
        out_specs=[ANY] * 8,
        scratch_shapes=[pltpu.SemaphoreType.DMA((32,))],
        name="split",
    )(keys, values)


def join_kernel(*refs):
    ins, (keys, values, sem) = refs[:8], refs[8:]
    copies = []
    for s, (dy, dc) in enumerate(SLOTS):
        for zh in range(2):
            for a, array in enumerate((keys, values)):
                copies.append(
                    pltpu.make_async_copy(
                        ins[s].at[a, zh],
                        array.at[:, slot_columns(dy, dc, zh)],
                        sem.at[len(copies)],
                    )
                )
    for copy in copies:
        copy.start()
    for copy in copies:
        copy.wait()


def join(chunks):
    return pl.pallas_call(
        join_kernel,
        out_shape=[jax.ShapeDtypeStruct((KEYS, HEADS * DH), BF16)] * 2,
        in_specs=[ANY] * 8,
        out_specs=[ANY] * 2,
        scratch_shapes=[pltpu.SemaphoreType.DMA((32,))],
        name="join",
    )(*chunks)


def dot(a, b, ca, cb):
    return lax.dot_general(a, b, (((ca,), (cb,)), ((), ())), preferred_element_type=F32)


def attention_kernel(*refs):
    messages, chunks = refs[:4], refs[4:12]
    grads, query_grads = refs[12:20], refs[20:24]
    kv, qt, dt, stat, dkv, dqt, ds, sem, out_sem = refs[24:]
    x = lax.axis_index("x")
    reads = []
    for k in range(4):
        j = lax.bitwise_xor(x, k)
        part = pl.ds(pl.multiple_of(j * PART, PART), PART)
        reads.append((messages[k].at[:, :PART, :], qt.at[:, part, :]))
        reads.append((messages[k].at[:, PART : 2 * PART, :], dt.at[:, part, :]))
        reads.append((messages[k].at[:, 2 * PART :, :], stat.at[k]))
    for s in range(8):
        reads.append((chunks[s], kv.at[s]))
    reads = [pltpu.make_async_copy(a, b, sem.at[i]) for i, (a, b) in enumerate(reads)]
    for copy in reads:
        copy.start()
    for copy in reads:
        copy.wait()

    writes = []

    def write(source, target):
        copy = pltpu.make_async_copy(source, target, out_sem.at[len(writes)])
        copy.start()
        writes.append(copy)

    for zh in range(2):
        sums, norms = [], []
        for zl in range(4):
            rows = [stat[k, 4 * zh + zl].astype(F32) for k in range(4)]
            total = rows[0] + rows[1] + rows[2] + rows[3]
            sums.append(total[0:1] + total[1:2] + total[2:3])
            norms.append((rows[0][3:4] + rows[0][4:5] + rows[0][5:6]) * LOG2E)

        for block in range(4):
            keys = kv[2 * block : 2 * block + 2, 0, zh].reshape(2 * KEYS, DH)
            values = kv[2 * block : 2 * block + 2, 1, zh].reshape(2 * KEYS, DH)
            weights, slopes = [], []
            for zl in range(4):
                z = 4 * zh + zl
                score = dot(keys, qt[z], 1, 0)
                weight = jnp.exp2(score * (FACTOR * LOG2E) - norms[zl])
                slope = dot(values, dt[z], 1, 0)
                grad = (weight * (slope - sums[zl])).astype(BF16)
                weights.append(weight.astype(BF16))
                slopes.append(grad)
                ds[zl, block * 2 * KEYS : (block + 1) * 2 * KEYS, :] = grad
            value_grad = sum(dot(weights[zl], dt[4 * zh + zl], 1, 1) for zl in range(4))
            key_grad = sum(dot(slopes[zl], qt[4 * zh + zl], 1, 1) for zl in range(4))
            for half in range(2):
                rows = slice(half * KEYS, (half + 1) * KEYS)
                dkv[2 * block + half, 0, zh] = (key_grad[rows] * FACTOR).astype(BF16)
                dkv[2 * block + half, 1, zh] = value_grad[rows].astype(BF16)
                if zh == 1:
                    write(dkv.at[2 * block + half], grads[2 * block + half])
        keys = kv[:, 0, zh].reshape(8 * KEYS, DH)
        for zl in range(4):
            dqt[4 * zh + zl] = (dot(keys, ds[zl], 0, 0) * FACTOR).astype(BF16)
    for k in range(4):
        j = lax.bitwise_xor(x, k)
        part = pl.ds(pl.multiple_of(j * PART, PART), PART)
        write(dqt.at[:, part, :], query_grads[k])
    for copy in writes:
        copy.wait()


def attention(messages, chunks):
    chunk = jax.ShapeDtypeStruct((2, 2, KEYS, DH), BF16)
    part = jax.ShapeDtypeStruct((8, PART, ROWS), BF16)
    outs = pl.pallas_call(
        attention_kernel,
        out_shape=[chunk] * 8 + [part] * 4,
        in_specs=[ANY] * 12,
        out_specs=[ANY] * 12,
        scratch_shapes=[
            pltpu.VMEM((8, 2, 2, KEYS, DH), BF16),
            pltpu.VMEM((8, DH, ROWS), BF16),
            pltpu.VMEM((8, DH, ROWS), BF16),
            pltpu.VMEM((4, 8, STAT, ROWS), BF16),
            pltpu.VMEM((8, 2, 2, KEYS, DH), BF16),
            pltpu.VMEM((8, DH, ROWS), BF16),
            pltpu.VMEM((4, 8 * KEYS, ROWS), BF16),
            pltpu.SemaphoreType.DMA((20,)),
            pltpu.SemaphoreType.DMA((12,)),
        ],
        compiler_params=pltpu.CompilerParams(vmem_limit_bytes=40 * 1024 * 1024),
        cost_estimate=pl.CostEstimate(
            flops=5 * 2 * 2 * 1024 * 1024 * 256,
            bytes_accessed=8 * 1024 * 1024,
            transcendentals=2 * 1024 * 1024,
        ),
        name="attention",
    )(*messages, *chunks)
    return outs[:8], outs[8:]


def local(queries, outputs, cotangent, log_norms, memory_keys, memory_values):
    chunks = split(memory_keys, memory_values)
    received = [chunks[0]] + [
        lax.ppermute(chunk, ("y", "core"), memory_pairs(*slot))
        for slot, chunk in list(zip(SLOTS, chunks))[1:]
    ]
    message = make_message(queries.T, outputs.T, cotangent.T, log_norms.T)
    gathered = lax.all_to_all(message, PLANE_Z, split_axis=0, concat_axis=0, tiled=True)
    messages = [lax.ppermute(gathered, ("x", "core"), plane_pairs(k)) for k in range(4)]
    grads, query_parts = attention(messages, received)
    query_parts = [
        lax.ppermute(part, ("x", "core"), inverse(plane_pairs(k)))
        for k, part in enumerate(query_parts)
    ]
    part = sum(p.astype(F32) for p in query_parts).astype(BF16)
    returned = [grads[0]] + [
        lax.ppermute(grad, ("y", "core"), inverse(memory_pairs(*slot)))
        for slot, grad in list(zip(SLOTS, grads))[1:]
    ]
    part = lax.all_to_all(part, PLANE_Z, split_axis=0, concat_axis=0, tiled=True)
    query_grads = jnp.sum(part.astype(F32), axis=0).astype(BF16).T
    key_grads, value_grads = join(returned)
    return query_grads, key_grads, value_grads


def solution(mesh):
    fine = Mesh(mesh.devices.reshape(SIZES), AXES)
    return jax.shard_map(
        local,
        mesh=fine,
        in_specs=(
            P("zl", MEM),
            P("zl", MEM),
            P("zl", MEM),
            P("zl", None),
            P(MEM + ("zl",), None),
            P(MEM + ("zl",), None),
        ),
        out_specs=(P("zl", MEM), P(MEM + ("zl",), None), P(MEM + ("zl",), None)),
        check_vma=False,
    )
```

```python
import jax
import jax.numpy as jnp
from jax import lax
from jax.experimental import pallas as pl
from jax.experimental.pallas import tpu as pltpu
from jax.sharding import Mesh, PartitionSpec as P

AXES = ("y", "zh", "x", "core", "zl")
SIZES = (4, 2, 4, 2, 4)
MEM = ("y", "zh", "x", "core")
PLANE_Z = ("zh", "zl")
HEADS = 16
DH = 256
ROWS = 256
PART = 64
KEYS = 128
STAT = 16
MESSAGE = 2 * PART + STAT
FACTOR = DH**-0.5
LOG2E = 1.4426950408889634
SLOTS = [(dy, dc) for dy in (0, 1, 2, 3) for dc in (0, 1)]
BF16, F32 = jnp.bfloat16, jnp.float32
ANY = pl.BlockSpec(memory_space=pl.ANY)
VMEM = pl.BlockSpec(memory_space=pltpu.VMEM)


def memory_pairs(dy, dc):
    return [
        (y * 2 + c, ((y + dy) % 4) * 2 + (c ^ dc)) for y in range(4) for c in range(2)
    ]


def plane_pairs(k):
    return [
        ((2 * xh + j // 2) * 2 + j % 2, (j ^ k) * 2 + xh)
        for xh in range(2)
        for j in range(4)
    ]


def inverse(pairs):
    return [(b, a) for a, b in pairs]


def pieces(value):
    high = value.astype(BF16)
    rest = value - high.astype(F32)
    middle = rest.astype(BF16)
    low = (rest - middle.astype(F32)).astype(BF16)
    return [high, middle, low]


def message_kernel(queries, outputs, cotangent, log_norms, message):
    sums = jnp.sum(
        cotangent[...].astype(F32) * outputs[...].astype(F32), axis=0, keepdims=True
    )
    zh, x, y = lax.axis_index("zh"), lax.axis_index("x"), lax.axis_index("y")
    head = 4 * y + 2 * zh + x // 2
    mine = lax.broadcasted_iota(jnp.int32, (HEADS, ROWS), 0) == head
    norms = jnp.sum(jnp.where(mine, log_norms[...], 0.0), axis=0, keepdims=True)
    rows = [r.astype(F32) for r in pieces(sums) + pieces(norms)]
    stat = jnp.concatenate(rows + [jnp.zeros((STAT - 6, ROWS), F32)], axis=0).astype(BF16)
    for z in range(8):
        message[z, :PART, :] = queries[...]
        message[z, PART : 2 * PART, :] = cotangent[...]
        message[z, 2 * PART :, :] = stat


def make_message(queries, outputs, cotangent, log_norms):
    return pl.pallas_call(
        message_kernel,
        out_shape=jax.ShapeDtypeStruct((8, MESSAGE, ROWS), BF16),
        in_specs=[VMEM] * 4,
        out_specs=VMEM,
        name="message",
    )(queries, outputs, cotangent, log_norms)


def slot_columns(dy, dc, zh):
    y, core = lax.axis_index("y"), lax.axis_index("core")
    owner = lax.rem(y + dy, 4)
    half = core if dc == 0 else 1 - core
    return pl.ds(pl.multiple_of((4 * owner + 2 * zh + half) * DH, DH), DH)


def split_kernel(keys, values, *refs):
    outs, sem = refs[:8], refs[8]
    copies = []
    for s, (dy, dc) in enumerate(SLOTS):
        for zh in range(2):
            for a, array in enumerate((keys, values)):
                copies.append(
                    pltpu.make_async_copy(
                        array.at[:, slot_columns(dy, dc, zh)],
                        outs[s].at[a, zh],
                        sem.at[len(copies)],
                    )
                )
    for copy in copies:
        copy.start()
    for copy in copies:
        copy.wait()


def split(keys, values):
    return pl.pallas_call(
        split_kernel,
        out_shape=[jax.ShapeDtypeStruct((2, 2, KEYS, DH), BF16)] * 8,
        in_specs=[VMEM] * 2,
        out_specs=[ANY] * 8,
        scratch_shapes=[pltpu.SemaphoreType.DMA((32,))],
        name="split",
    )(keys, values)


def join_kernel(*refs):
    ins, (keys, values, sem) = refs[:8], refs[8:]
    copies = []
    for s, (dy, dc) in enumerate(SLOTS):
        for zh in range(2):
            for a, array in enumerate((keys, values)):
                copies.append(
                    pltpu.make_async_copy(
                        ins[s].at[a, zh],
                        array.at[:, slot_columns(dy, dc, zh)],
                        sem.at[len(copies)],
                    )
                )
    for copy in copies:
        copy.start()
    for copy in copies:
        copy.wait()


def join(chunks):
    return pl.pallas_call(
        join_kernel,
        out_shape=[jax.ShapeDtypeStruct((KEYS, HEADS * DH), BF16)] * 2,
        in_specs=[ANY] * 8,
        out_specs=[VMEM] * 2,
        scratch_shapes=[pltpu.SemaphoreType.DMA((32,))],
        name="join",
    )(*chunks)


def dot(a, b, ca, cb):
    return lax.dot_general(a, b, (((ca,), (cb,)), ((), ())), preferred_element_type=F32)


def attention_kernel(*refs):
    messages, chunks = refs[:4], refs[4:12]
    grads, query_grads = refs[12:20], refs[20:24]
    kv, qt, dt, stat, dkv, dqt, ds, sem, out_sem = refs[24:]
    x = lax.axis_index("x")
    reads = []
    for k in range(4):
        j = lax.bitwise_xor(x, k)
        part = pl.ds(pl.multiple_of(j * PART, PART), PART)
        reads.append((messages[k].at[:, :PART, :], qt.at[:, part, :]))
        reads.append((messages[k].at[:, PART : 2 * PART, :], dt.at[:, part, :]))
        reads.append((messages[k].at[:, 2 * PART :, :], stat.at[k]))
    for s in range(8):
        reads.append((chunks[s], kv.at[s]))
    reads = [pltpu.make_async_copy(a, b, sem.at[i]) for i, (a, b) in enumerate(reads)]
    for copy in reads:
        copy.start()
    for copy in reads:
        copy.wait()

    writes = []

    def write(source, target):
        copy = pltpu.make_async_copy(source, target, out_sem.at[len(writes)])
        copy.start()
        writes.append(copy)

    for zh in range(2):
        sums, norms = [], []
        for zl in range(4):
            rows = [stat[k, 4 * zh + zl].astype(F32) for k in range(4)]
            total = rows[0] + rows[1] + rows[2] + rows[3]
            sums.append(total[0:1] + total[1:2] + total[2:3])
            norms.append((rows[0][3:4] + rows[0][4:5] + rows[0][5:6]) * LOG2E)

        for block in range(4):
            keys = kv[2 * block : 2 * block + 2, 0, zh].reshape(2 * KEYS, DH)
            values = kv[2 * block : 2 * block + 2, 1, zh].reshape(2 * KEYS, DH)
            weights, slopes = [], []
            for zl in range(4):
                z = 4 * zh + zl
                score = dot(keys, qt[z], 1, 0)
                weight = jnp.exp2(score * (FACTOR * LOG2E) - norms[zl])
                slope = dot(values, dt[z], 1, 0)
                grad = (weight * (slope - sums[zl])).astype(BF16)
                weights.append(weight.astype(BF16))
                slopes.append(grad)
                ds[zl, block * 2 * KEYS : (block + 1) * 2 * KEYS, :] = grad
            value_grad = sum(dot(weights[zl], dt[4 * zh + zl], 1, 1) for zl in range(4))
            key_grad = sum(dot(slopes[zl], qt[4 * zh + zl], 1, 1) for zl in range(4))
            for half in range(2):
                rows = slice(half * KEYS, (half + 1) * KEYS)
                dkv[2 * block + half, 0, zh] = (key_grad[rows] * FACTOR).astype(BF16)
                dkv[2 * block + half, 1, zh] = value_grad[rows].astype(BF16)
                if zh == 1:
                    write(dkv.at[2 * block + half], grads[2 * block + half])
        keys = kv[:, 0, zh].reshape(8 * KEYS, DH)
        for zl in range(4):
            dqt[4 * zh + zl] = (dot(keys, ds[zl], 0, 0) * FACTOR).astype(BF16)
    for k in range(4):
        j = lax.bitwise_xor(x, k)
        part = pl.ds(pl.multiple_of(j * PART, PART), PART)
        write(dqt.at[:, part, :], query_grads[k])
    for copy in writes:
        copy.wait()


def attention(messages, chunks):
    chunk = jax.ShapeDtypeStruct((2, 2, KEYS, DH), BF16)
    part = jax.ShapeDtypeStruct((8, PART, ROWS), BF16)
    outs = pl.pallas_call(
        attention_kernel,
        out_shape=[chunk] * 8 + [part] * 4,
        in_specs=[ANY] * 12,
        out_specs=[ANY] * 12,
        scratch_shapes=[
            pltpu.VMEM((8, 2, 2, KEYS, DH), BF16),
            pltpu.VMEM((8, DH, ROWS), BF16),
            pltpu.VMEM((8, DH, ROWS), BF16),
            pltpu.VMEM((4, 8, STAT, ROWS), BF16),
            pltpu.VMEM((8, 2, 2, KEYS, DH), BF16),
            pltpu.VMEM((8, DH, ROWS), BF16),
            pltpu.VMEM((4, 8 * KEYS, ROWS), BF16),
            pltpu.SemaphoreType.DMA((20,)),
            pltpu.SemaphoreType.DMA((12,)),
        ],
        compiler_params=pltpu.CompilerParams(vmem_limit_bytes=40 * 1024 * 1024),
        cost_estimate=pl.CostEstimate(
            flops=5 * 2 * 2 * 1024 * 1024 * 256,
            bytes_accessed=8 * 1024 * 1024,
            transcendentals=2 * 1024 * 1024,
        ),
        name="attention",
    )(*messages, *chunks)
    return outs[:8], outs[8:]


def local(queries, outputs, cotangent, log_norms, memory_keys, memory_values):
    chunks = split(memory_keys, memory_values)
    received = [chunks[0]] + [
        lax.ppermute(chunk, ("y", "core"), memory_pairs(*slot))
        for slot, chunk in list(zip(SLOTS, chunks))[1:]
    ]
    message = make_message(queries.T, outputs.T, cotangent.T, log_norms.T)
    gathered = lax.all_to_all(message, PLANE_Z, split_axis=0, concat_axis=0, tiled=True)
    messages = [lax.ppermute(gathered, ("x", "core"), plane_pairs(k)) for k in range(4)]
    grads, query_parts = attention(messages, received)
    query_parts = [
        lax.ppermute(part, ("x", "core"), inverse(plane_pairs(k)))
        for k, part in enumerate(query_parts)
    ]
    part = sum(p.astype(F32) for p in query_parts).astype(BF16)
    returned = [grads[0]] + [
        lax.ppermute(grad, ("y", "core"), inverse(memory_pairs(*slot)))
        for slot, grad in list(zip(SLOTS, grads))[1:]
    ]
    part = lax.all_to_all(part, PLANE_Z, split_axis=0, concat_axis=0, tiled=True)
    query_grads = jnp.sum(part.astype(F32), axis=0).astype(BF16).T
    key_grads, value_grads = join(returned)
    return query_grads, key_grads, value_grads


def solution(mesh):
    fine = Mesh(mesh.devices.reshape(SIZES), AXES)
    return jax.shard_map(
        local,
        mesh=fine,
        in_specs=(
            P("zl", MEM),
            P("zl", MEM),
            P("zl", MEM),
            P("zl", None),
            P(MEM + ("zl",), None),
            P(MEM + ("zl",), None),
        ),
        out_specs=(P("zl", MEM), P(MEM + ("zl",), None), P(MEM + ("zl",), None)),
        check_vma=False,
    )
```

```python
import jax
import jax.numpy as jnp
from jax import lax
from jax.experimental import pallas as pl
from jax.experimental.pallas import tpu as pltpu
from jax.sharding import Mesh, PartitionSpec as P

AXES = ("y", "zh", "x", "core", "zl")
SIZES = (4, 2, 4, 2, 4)
MEM = ("y", "zh", "x", "core")
OWNERS = ("y", "x")
HEADS = 16
DH = 256
ROWS = 256
PART = 64
KEYS = 128
STAT = 16
FACTOR = DH**-0.5
LOG2E = 1.4426950408889634
MIB = 1024 * 1024
BF16, F32 = jnp.bfloat16, jnp.float32
HBM = pl.BlockSpec(memory_space=pltpu.HBM)
VMEM = pl.BlockSpec(memory_space=pltpu.VMEM)


def call(kernel, outs, ins, out_specs, limit, name, scratch=(), cost=None):
    return pl.pallas_call(
        kernel,
        out_shape=outs,
        in_specs=ins,
        out_specs=out_specs,
        scratch_shapes=list(scratch),
        compiler_params=pltpu.CompilerParams(vmem_limit_bytes=limit * MIB),
        cost_estimate=cost,
        name=name,
    )


def shape(*dims, dtype=BF16):
    return jax.ShapeDtypeStruct(dims, dtype)


def pair_of(zh, x):
    return zh * 4 + x


CROSS = [
    (pair_of(zh, x), pair_of(zh, x - 1) if x % 2 else pair_of(1 - zh, x + 1))
    for zh in range(2)
    for x in range(4)
]
STRAIGHT = [
    (pair_of(zh, x), pair_of(1 - zh, x) if x % 2 else pair_of(zh, x))
    for zh in range(2)
    for x in range(4)
]
SWAP = [(0, 1), (1, 0)]


def inverse(pairs):
    return [(b, a) for a, b in pairs]


def turn(step):
    return [(i, (i + step) % 4) for i in range(4)]


def pieces(value):
    high = value.astype(BF16)
    rest = value - high.astype(F32)
    middle = rest.astype(BF16)
    low = (rest - middle.astype(F32)).astype(BF16)
    return [high.astype(F32), middle.astype(F32), low.astype(F32)]


def in_hbm(array):
    return pltpu.with_memory_space_constraint(array, pltpu.HBM)


def stat_rows(rows):
    pad = jnp.zeros((STAT - 6, ROWS), F32)
    return jnp.concatenate(rows + [pad], axis=0).astype(BF16)


def message_kernel(*refs):
    message, scratch, sem = refs[4], refs[5:9], refs[9]
    copies = [
        pltpu.make_async_copy(refs[i], scratch[i], sem.at[i]) for i in range(4)
    ]
    for copy in copies:
        copy.start()
    for copy in copies:
        copy.wait()
    queries, outputs, cotangent, log_norms = scratch
    sums = jnp.sum(
        cotangent[...].astype(F32) * outputs[...].astype(F32), axis=0, keepdims=True
    )
    zh, x, y = lax.axis_index("zh"), lax.axis_index("x"), lax.axis_index("y")
    head = 4 * y + 2 * zh + x // 2
    mine = lax.broadcasted_iota(jnp.int32, (HEADS, ROWS), 0) == head
    norms = jnp.sum(jnp.where(mine, log_norms[...], 0.0), axis=0, keepdims=True)
    message[:PART, :] = queries[...]
    message[PART : 2 * PART, :] = cotangent[...]
    message[2 * PART :, :] = stat_rows(pieces(sums) + pieces(norms))


def make_message(*args):
    return call(
        message_kernel,
        shape(2 * PART + STAT, ROWS),
        [HBM] * 4,
        VMEM,
        4,
        "message",
        [pltpu.VMEM(a.shape, a.dtype) for a in args] + [pltpu.SemaphoreType.DMA((4,))],
    )(*map(in_hbm, args))


def bundle_kernel(cross, straight, out):
    odd = lax.rem(lax.axis_index("x"), 2)
    for ref, place in ((cross, 1 - odd), (straight, odd)):
        start = pl.multiple_of(place * PART, PART)
        out[pl.ds(start, PART), :] = ref[:PART, :]
        out[pl.ds(start + 2 * PART, PART), :] = ref[PART : 2 * PART, :]
    one, two = cross[2 * PART :, :].astype(F32), straight[2 * PART :, :].astype(F32)
    both = one + two
    rows = pieces(both[0:1] + both[1:2] + both[2:3])
    out[4 * PART :, :] = stat_rows(rows + [one[3:6]])


def bundle(*args):
    return call(
        bundle_kernel, shape(4 * PART + STAT, ROWS), [VMEM] * 2, VMEM, 4, "bundle"
    )(*args)


def stack_kernel(*refs):
    for i, ref in enumerate(refs[:-1]):
        refs[-1][i] = ref[...]


def stack(parts):
    out = shape(len(parts), *parts[0].shape)
    return call(stack_kernel, out, [VMEM] * len(parts), VMEM, 8, "stack")(*parts)


def slot_columns(s):
    y, x = s // 4, s % 4
    zh = lax.axis_index("zh")
    if x % 2:
        zh = 1 - zh
    return pl.ds(pl.multiple_of((4 * y + 2 * zh + x // 2) * DH, DH), DH)


def split_kernel(keys, values, out, held, in_sem, out_sem):
    pieces = [(s, a) for s in range(16) for a in range(2)]
    reads, writes = [], []
    for s, a in pieces:
        array = (keys, values)[a]
        at = held.at[s, a]
        number = 2 * s + a
        reads.append(
            pltpu.make_async_copy(array.at[:, slot_columns(s)], at, in_sem.at[number])
        )
        writes.append(pltpu.make_async_copy(at, out.at[s, a], out_sem.at[number]))
    for copy in reads:
        copy.start()
    for read, write in zip(reads, writes):
        read.wait()
        write.start()
    for copy in writes:
        copy.wait()


def split(keys, values):
    return call(
        split_kernel,
        pltpu.HBM((16, 2, KEYS, DH), BF16),
        [HBM] * 2,
        HBM,
        8,
        "split",
        [
            pltpu.VMEM((16, 2, KEYS, DH), BF16),
            pltpu.SemaphoreType.DMA((32,)),
            pltpu.SemaphoreType.DMA((32,)),
        ],
        pl.CostEstimate(flops=0, bytes_accessed=8 * MIB, transcendentals=0),
    )(in_hbm(keys), in_hbm(values))


def join_kernel(chunks, keys, values):
    for s in range(16):
        columns = slot_columns(s)
        keys[:, columns] = chunks[s, 0]
        values[:, columns] = chunks[s, 1]


def join(chunks):
    out = shape(KEYS, HEADS * DH)
    return call(join_kernel, [out] * 2, [VMEM], [VMEM] * 2, 8, "join")(chunks)


def dot(a, b, ca, cb):
    return lax.dot_general(a, b, (((ca,), (cb,)), ((), ())), preferred_element_type=F32)


def attention_kernel(
    mine, there, kv, grads, own, other, theirs, qt, dt, stat, dkv, dq, ds, sem
):
    core, here = lax.axis_index("core"), lax.axis_index("zl")
    copy = pltpu.make_async_copy(there, theirs, sem.at[0])
    copy.start()
    copy.wait()
    for d in range(4):
        zl = lax.rem(here + 4 - d, 4)
        for ref, c in ((mine, core), (theirs, 1 - core)):
            for xl in range(2):
                to = pl.ds(pl.multiple_of((2 * xl + c) * PART, PART), PART)
                qt[zl, to, :] = ref[d, xl * PART : (xl + 1) * PART, :]
                dt[zl, to, :] = ref[d, (2 + xl) * PART : (3 + xl) * PART, :]
        one = mine[d, 4 * PART :, :].astype(F32)
        both = one + theirs[d, 4 * PART :, :].astype(F32)
        stat[zl, 0:1, :] = both[0:1] + both[1:2] + both[2:3]
        stat[zl, 1:2, :] = (one[3:4] + one[4:5] + one[5:6]) * LOG2E

    writes = []
    for block in range(8):
        rows = slice(block * 2 * KEYS, (block + 1) * 2 * KEYS)
        keys = kv[2 * block : 2 * block + 2, 0].reshape(2 * KEYS, DH)
        values = kv[2 * block : 2 * block + 2, 1].reshape(2 * KEYS, DH)
        weights, slopes = [], []
        for zl in range(4):
            score = dot(keys, qt[zl], 1, 0)
            weight = jnp.exp2(score * (FACTOR * LOG2E) - stat[zl, 1:2, :])
            slope = dot(values, dt[zl], 1, 0)
            grad = (weight * (slope - stat[zl, 0:1, :])).astype(BF16)
            weights.append(weight.astype(BF16))
            slopes.append(grad)
            ds[zl, rows, :] = grad
        value_grad = sum(dot(weights[zl], dt[zl], 1, 1) for zl in range(4))
        key_grad = sum(dot(slopes[zl], qt[zl], 1, 1) for zl in range(4)) * FACTOR
        for half in range(2):
            part = slice(half * KEYS, (half + 1) * KEYS)
            dkv[2 * block + half, 0] = key_grad[part].astype(BF16)
            dkv[2 * block + half, 1] = value_grad[part].astype(BF16)
        pair = slice(2 * block, 2 * block + 2)
        copy = pltpu.make_async_copy(dkv.at[pair], grads.at[pair], sem.at[block])
        copy.start()
        writes.append(copy)
    keys = kv[:, 0].reshape(16 * KEYS, DH)
    for zl in range(4):
        dq[zl] = dot(keys, ds[zl], 0, 0) * FACTOR
    for d in range(4):
        zl = lax.rem(here + d, 4)
        for xl in range(2):
            at = pl.ds(pl.multiple_of((2 * xl + core) * PART, PART), PART)
            own[d, xl] = dq[zl, at, :]
            at = pl.ds(pl.multiple_of((2 * xl + 1 - core) * PART, PART), PART)
            other[d, xl] = dq[zl, at, :].astype(BF16)
    for copy in writes:
        copy.wait()


def attention(mine, theirs, kv):
    part = (4, 2, PART, ROWS)
    return call(
        attention_kernel,
        [pltpu.HBM((16, 2, KEYS, DH), BF16), shape(*part, dtype=F32), shape(*part)],
        [VMEM, HBM, VMEM],
        [HBM, VMEM, VMEM],
        32,
        "attention",
        [
            pltpu.VMEM((4, 4 * PART + STAT, ROWS), BF16),
            pltpu.VMEM((4, DH, ROWS), BF16),
            pltpu.VMEM((4, DH, ROWS), BF16),
            pltpu.VMEM((4, 8, ROWS), F32),
            pltpu.VMEM((16, 2, KEYS, DH), BF16),
            pltpu.VMEM((4, DH, ROWS), F32),
            pltpu.VMEM((4, 16 * KEYS, ROWS), BF16),
            pltpu.SemaphoreType.DMA((8,)),
        ],
        pl.CostEstimate(
            flops=5 * 2 * 2048 * 1024 * 256,
            bytes_accessed=8 * MIB,
            transcendentals=2048 * 1024,
        ),
    )(mine, in_hbm(theirs), kv)


def core_sum_kernel(own, other, *outs):
    for d, out in enumerate(outs):
        out[...] = (own[d] + other[d].astype(F32)).astype(BF16)


def core_sum(own, other):
    return call(
        core_sum_kernel,
        [shape(2, PART, ROWS)] * 4,
        [VMEM] * 2,
        [VMEM] * 4,
        4,
        "core_sum",
    )(own, other)


def line_sum_kernel(*refs):
    parts, cross, straight = refs[:4], refs[4], refs[5]
    odd = lax.rem(lax.axis_index("x"), 2)
    for out, place in ((cross, 1 - odd), (straight, odd)):
        total = parts[0][place].astype(F32)
        for part in parts[1:]:
            total = total + part[place].astype(F32)
        out[...] = total.astype(BF16)


def line_sum(parts):
    return call(
        line_sum_kernel, [shape(PART, ROWS)] * 2, [VMEM] * 4, [VMEM] * 2, 4, "line_sum"
    )(*parts)


def local(queries, outputs, cotangent, log_norms, memory_keys, memory_values):
    message = make_message(queries.T, outputs.T, cotangent.T, log_norms.T)
    cross = lax.ppermute(message, ("zh", "x"), CROSS)
    straight = lax.ppermute(message, ("zh", "x"), STRAIGHT)
    chunks = split(memory_keys, memory_values)
    chunks, cross, straight = lax.optimization_barrier((chunks, cross, straight))
    received = lax.all_to_all(chunks, OWNERS, split_axis=0, concat_axis=0, tiled=True)
    first = bundle(cross, straight)
    mine = stack([first] + [lax.ppermute(first, "zl", turn(d)) for d in (1, 2, 3)])
    theirs = lax.ppermute(mine, "core", SWAP)
    grads, own, other = attention(mine, theirs, received)
    returned = lax.all_to_all(grads, OWNERS, split_axis=0, concat_axis=0, tiled=True)
    sums = core_sum(own, lax.ppermute(other, "core", SWAP))
    parts = [sums[0]] + [lax.ppermute(sums[d], "zl", turn(d)) for d in (1, 2, 3)]
    cross, straight = line_sum(parts)
    cross = lax.ppermute(cross, ("zh", "x"), inverse(CROSS))
    straight = lax.ppermute(straight, ("zh", "x"), inverse(STRAIGHT))
    query_grads = (cross.astype(F32) + straight.astype(F32)).astype(BF16).T
    key_grads, value_grads = join(returned)
    return query_grads, key_grads, value_grads


def solution(mesh):
    fine = Mesh(mesh.devices.reshape(SIZES), AXES)
    return jax.shard_map(
        local,
        mesh=fine,
        in_specs=(
            P("zl", MEM),
            P("zl", MEM),
            P("zl", MEM),
            P("zl", None),
            P(MEM + ("zl",), None),
            P(MEM + ("zl",), None),
        ),
        out_specs=(P("zl", MEM), P(MEM + ("zl",), None), P(MEM + ("zl",), None)),
        check_vma=False,
    )
```

```python
import jax
import jax.numpy as jnp
from jax import lax
from jax.experimental import pallas as pl
from jax.experimental.pallas import tpu as pltpu
from jax.sharding import Mesh, PartitionSpec as P

AXES = ("y", "zh", "x", "core", "zl")
SIZES = (4, 2, 4, 2, 4)
MEM = ("y", "zh", "x", "core")
HEADS = 16
DH = 256
ROWS = 256
PART = 64
KEYS = 128
STAT = 16
FACTOR = DH**-0.5
LOG2E = 1.4426950408889634
MIB = 1024 * 1024
BF16, F32 = jnp.bfloat16, jnp.float32
HBM = pl.BlockSpec(memory_space=pltpu.HBM)
VMEM = pl.BlockSpec(memory_space=pltpu.VMEM)


def call(kernel, outs, ins, out_specs, limit, name, scratch=(), cost=None):
    return pl.pallas_call(
        kernel,
        out_shape=outs,
        in_specs=ins,
        out_specs=out_specs,
        scratch_shapes=list(scratch),
        compiler_params=pltpu.CompilerParams(vmem_limit_bytes=limit * MIB),
        cost_estimate=cost,
        name=name,
    )


def shape(*dims, dtype=BF16):
    return jax.ShapeDtypeStruct(dims, dtype)


LINE = ("zh", "x", "zl")


def line_pairs(k):
    pairs = []
    for zh in range(2):
        for x in range(4):
            for zl in range(4):
                z = 2 * ((zl + k) % 4) + (zh + x) % 2
                to = (z // 4 * 4 + x) * 4 + z % 4
                pairs.append(((zh * 4 + x) * 4 + zl, to))
    return pairs


def row_block(k):
    step = 2 * lax.axis_index("zh") + lax.axis_index("zl") // 2
    return lax.rem(step + 4 - k, 4)


NEXT = [(0, 1), (1, 0), (2, 3), (3, 2)]
SWAP = [(0, 1), (1, 0)]


def peer(slot, core):
    return (slot // 4 + 2 * core) % 4, (slot + 2 * core) % 4


def exchange(chunks):
    groups = []
    for zh in range(2):
        for core in range(2):
            for zl in range(4):
                peers = [peer(slot, core) for slot in range(16)]
                groups.append(
                    [(((y * 2 + zh) * 4 + x) * 2 + core) * 4 + zl for y, x in peers]
                )
    return lax.all_to_all(
        chunks, AXES, split_axis=0, concat_axis=0, tiled=True, axis_index_groups=groups
    )


def inverse(pairs):
    return [(b, a) for a, b in pairs]


def pieces(value):
    high = value.astype(BF16)
    rest = value - high.astype(F32)
    middle = rest.astype(BF16)
    low = (rest - middle.astype(F32)).astype(BF16)
    return [high.astype(F32), middle.astype(F32), low.astype(F32)]


def in_hbm(array):
    return pltpu.with_memory_space_constraint(array, pltpu.HBM)


def stat_rows(rows):
    pad = jnp.zeros((STAT - 6, ROWS), F32)
    return jnp.concatenate(rows + [pad], axis=0).astype(BF16)


def message_kernel(*refs):
    message, scratch, sem = refs[4], refs[5:9], refs[9]
    copies = [
        pltpu.make_async_copy(refs[i], scratch[i], sem.at[i]) for i in range(4)
    ]
    for copy in copies:
        copy.start()
    for copy in copies:
        copy.wait()
    queries, outputs, cotangent, log_norms = scratch
    sums = jnp.sum(
        cotangent[...].astype(F32) * outputs[...].astype(F32), axis=0, keepdims=True
    )
    zh, x, y = lax.axis_index("zh"), lax.axis_index("x"), lax.axis_index("y")
    head = 4 * y + 2 * zh + x // 2
    mine = lax.broadcasted_iota(jnp.int32, (HEADS, ROWS), 0) == head
    norms = jnp.sum(jnp.where(mine, log_norms[...], 0.0), axis=0, keepdims=True)
    message[:PART, :] = queries[...]
    message[PART : 2 * PART, :] = cotangent[...]
    message[2 * PART :, :] = stat_rows(pieces(sums) + pieces(norms))


def make_message(*args):
    return call(
        message_kernel,
        shape(2 * PART + STAT, ROWS),
        [HBM] * 4,
        VMEM,
        4,
        "message",
        [pltpu.VMEM(a.shape, a.dtype) for a in args] + [pltpu.SemaphoreType.DMA((4,))],
    )(*map(in_hbm, args))


def bundle_kernel(own, other, out):
    odd = lax.rem(lax.axis_index("x"), 2)
    for ref, place in ((own, odd), (other, 1 - odd)):
        start = pl.multiple_of(place * PART, PART)
        out[pl.ds(start, PART), :] = ref[:PART, :]
        out[pl.ds(start + 2 * PART, PART), :] = ref[PART : 2 * PART, :]
    one, two = own[2 * PART :, :].astype(F32), other[2 * PART :, :].astype(F32)
    both = one + two
    rows = pieces(both[0:1] + both[1:2] + both[2:3])
    out[4 * PART :, :] = stat_rows(rows + [one[3:6]])


def bundle(*args):
    return call(
        bundle_kernel, shape(4 * PART + STAT, ROWS), [VMEM] * 2, VMEM, 4, "bundle"
    )(*args)


def slot_columns(s):
    y, x = peer(s, lax.axis_index("core"))
    zh = (lax.axis_index("zl") + x) % 2
    return pl.ds(pl.multiple_of((4 * y + 2 * zh + x // 2) * DH, DH), DH)


def split_kernel(keys, values, out, held, in_sem, out_sem):
    pieces = [(s, a) for s in range(16) for a in range(2)]
    reads, writes = [], []
    for s, a in pieces:
        array = (keys, values)[a]
        at = held.at[s, a]
        number = 2 * s + a
        reads.append(
            pltpu.make_async_copy(array.at[:, slot_columns(s)], at, in_sem.at[number])
        )
        writes.append(pltpu.make_async_copy(at, out.at[s, a], out_sem.at[number]))
    for copy in reads:
        copy.start()
    for read, write in zip(reads, writes):
        read.wait()
        write.start()
    for copy in writes:
        copy.wait()


def split(keys, values):
    return call(
        split_kernel,
        pltpu.HBM((16, 2, KEYS, DH), BF16),
        [HBM] * 2,
        HBM,
        8,
        "split",
        [
            pltpu.VMEM((16, 2, KEYS, DH), BF16),
            pltpu.SemaphoreType.DMA((32,)),
            pltpu.SemaphoreType.DMA((32,)),
        ],
        pl.CostEstimate(flops=0, bytes_accessed=8 * MIB, transcendentals=0),
    )(in_hbm(keys), in_hbm(values))


def join_kernel(chunks, keys, values):
    for s in range(16):
        columns = slot_columns(s)
        keys[:, columns] = chunks[s, 0]
        values[:, columns] = chunks[s, 1]


def join(chunks):
    out = shape(KEYS, HEADS * DH)
    return call(join_kernel, [out] * 2, [VMEM], [VMEM] * 2, 8, "join")(chunks)


def dot(a, b, ca, cb):
    return lax.dot_general(a, b, (((ca,), (cb,)), ((), ())), preferred_element_type=F32)


def assemble_kernel(*refs):
    mine, theirs, (qt, dt, stat) = refs[:4], refs[4:8], refs[8:]
    core = lax.axis_index("core")
    for k in range(4):
        zl = row_block(k)
        for ref, c in ((mine[k], core), (theirs[k], 1 - core)):
            for xl in range(2):
                to = pl.ds(pl.multiple_of((2 * xl + c) * PART, PART), PART)
                qt[zl, to, :] = ref[xl * PART : (xl + 1) * PART, :]
                dt[zl, to, :] = ref[(2 + xl) * PART : (3 + xl) * PART, :]
        one = mine[k][4 * PART :, :].astype(F32)
        both = one + theirs[k][4 * PART :, :].astype(F32)
        stat[zl, 0:1, :] = both[0:1] + both[1:2] + both[2:3]
        stat[zl, 1:2, :] = (one[3:4] + one[4:5] + one[5:6]) * LOG2E


def assemble(mine, theirs):
    block = shape(4, DH, ROWS)
    return call(
        assemble_kernel,
        [block, block, shape(4, 8, ROWS, dtype=F32)],
        [VMEM] * 8,
        [VMEM] * 3,
        8,
        "assemble",
    )(*mine, *theirs)


def attention_kernel(qt, dt, stat, kv, grads, own, other, dkv, dq, ds, sem):
    core = lax.axis_index("core")
    writes = []
    for block in range(8):
        rows = slice(block * 2 * KEYS, (block + 1) * 2 * KEYS)
        keys = kv[2 * block : 2 * block + 2, 0].reshape(2 * KEYS, DH)
        values = kv[2 * block : 2 * block + 2, 1].reshape(2 * KEYS, DH)
        weights, slopes = [], []
        for zl in range(4):
            score = dot(keys, qt[zl], 1, 0)
            weight = jnp.exp2(score * (FACTOR * LOG2E) - stat[zl, 1:2, :])
            slope = dot(values, dt[zl], 1, 0)
            grad = (weight * (slope - stat[zl, 0:1, :])).astype(BF16)
            weights.append(weight.astype(BF16))
            slopes.append(grad)
            ds[zl, rows, :] = grad
        value_grad = sum(dot(weights[zl], dt[zl], 1, 1) for zl in range(4))
        key_grad = sum(dot(slopes[zl], qt[zl], 1, 1) for zl in range(4)) * FACTOR
        for half in range(2):
            part = slice(half * KEYS, (half + 1) * KEYS)
            dkv[2 * block + half, 0] = key_grad[part].astype(BF16)
            dkv[2 * block + half, 1] = value_grad[part].astype(BF16)
        pair = slice(2 * block, 2 * block + 2)
        copy = pltpu.make_async_copy(dkv.at[pair], grads.at[pair], sem.at[block])
        copy.start()
        writes.append(copy)
    keys = kv[:, 0].reshape(16 * KEYS, DH)
    for zl in range(4):
        dq[zl] = dot(keys, ds[zl], 0, 0) * FACTOR
    for k in range(4):
        zl = row_block(k)
        for xl in range(2):
            at = pl.ds(pl.multiple_of((2 * xl + core) * PART, PART), PART)
            own[k, xl] = dq[zl, at, :]
            at = pl.ds(pl.multiple_of((2 * xl + 1 - core) * PART, PART), PART)
            other[k, xl] = dq[zl, at, :].astype(BF16)
    for copy in writes:
        copy.wait()


def attention(qt, dt, stat, kv):
    part = (4, 2, PART, ROWS)
    return call(
        attention_kernel,
        [pltpu.HBM((16, 2, KEYS, DH), BF16), shape(*part, dtype=F32), shape(*part)],
        [VMEM] * 4,
        [HBM, VMEM, VMEM],
        32,
        "attention",
        [
            pltpu.VMEM((16, 2, KEYS, DH), BF16),
            pltpu.VMEM((4, DH, ROWS), F32),
            pltpu.VMEM((4, 16 * KEYS, ROWS), BF16),
            pltpu.SemaphoreType.DMA((8,)),
        ],
        pl.CostEstimate(
            flops=5 * 2 * 2048 * 1024 * 256,
            bytes_accessed=8 * MIB,
            transcendentals=2048 * 1024,
        ),
    )(qt, dt, stat, kv)


def core_sum_kernel(own, other, *outs):
    for d, out in enumerate(outs):
        out[...] = (own[d] + other[d].astype(F32)).astype(BF16)


def core_sum(own, other):
    return call(
        core_sum_kernel,
        [shape(2, PART, ROWS)] * 4,
        [VMEM] * 2,
        [VMEM] * 4,
        4,
        "core_sum",
    )(own, other)


def line_sum_kernel(*refs):
    parts, own, other = refs[:4], refs[4], refs[5]
    odd = lax.rem(lax.axis_index("x"), 2)
    for out, place in ((own, odd), (other, 1 - odd)):
        total = parts[0][place].astype(F32)
        for part in parts[1:]:
            total = total + part[place].astype(F32)
        out[...] = total.astype(out.dtype)


def line_sum(parts):
    outs = [shape(PART, ROWS, dtype=F32), shape(PART, ROWS)]
    return call(line_sum_kernel, outs, [VMEM] * 4, [VMEM] * 2, 4, "line_sum")(*parts)


def local(queries, outputs, cotangent, log_norms, memory_keys, memory_values):
    message = make_message(queries.T, outputs.T, cotangent.T, log_norms.T)
    other = lax.ppermute(message, "x", NEXT)
    chunks = split(memory_keys, memory_values)
    chunks, other = lax.optimization_barrier((chunks, other))
    received = exchange(chunks)
    part = bundle(message, other)
    mine = [lax.ppermute(part, LINE, line_pairs(k)) for k in range(4)]
    theirs = [lax.ppermute(part, "core", SWAP) for part in mine]
    grads, own, other = attention(*assemble(mine, theirs), received)
    returned = exchange(grads)
    sums = core_sum(own, lax.ppermute(other, "core", SWAP))
    sums = [lax.ppermute(sums[k], LINE, inverse(line_pairs(k))) for k in range(4)]
    own, other = line_sum(sums)
    other = lax.ppermute(other, "x", NEXT)
    key_grads, value_grads = join(returned)
    other, key_grads, value_grads = lax.optimization_barrier(
        (other, key_grads, value_grads)
    )
    query_grads = (own + other.astype(F32)).astype(BF16).T
    return query_grads, key_grads, value_grads


def solution(mesh):
    fine = Mesh(mesh.devices.reshape(SIZES), AXES)
    return jax.shard_map(
        local,
        mesh=fine,
        in_specs=(
            P("zl", MEM),
            P("zl", MEM),
            P("zl", MEM),
            P("zl", None),
            P(MEM + ("zl",), None),
            P(MEM + ("zl",), None),
        ),
        out_specs=(P("zl", MEM), P(MEM + ("zl",), None), P(MEM + ("zl",), None)),
        check_vma=False,
    )
```

```python
import jax
import jax.numpy as jnp
from jax import lax
from jax.experimental import pallas as pl
from jax.experimental.pallas import tpu as pltpu
from jax.sharding import Mesh, PartitionSpec as P

AXES = ("y", "zh", "x", "core", "zl")
SIZES = (4, 2, 4, 2, 4)
MEM = ("y", "zh", "x", "core")
HEADS = 16
DH = 256
ROWS = 256
PART = 64
KEYS = 128
STAT = 16
FACTOR = DH**-0.5
LOG2E = 1.4426950408889634
MIB = 1024 * 1024
BF16, F32 = jnp.bfloat16, jnp.float32
HBM = pl.BlockSpec(memory_space=pltpu.HBM)
VMEM = pl.BlockSpec(memory_space=pltpu.VMEM)


def call(kernel, outs, ins, out_specs, limit, name, scratch=(), cost=None):
    return pl.pallas_call(
        kernel,
        out_shape=outs,
        in_specs=ins,
        out_specs=out_specs,
        scratch_shapes=list(scratch),
        compiler_params=pltpu.CompilerParams(vmem_limit_bytes=limit * MIB),
        cost_estimate=cost,
        name=name,
    )


def shape(*dims, dtype=BF16):
    return jax.ShapeDtypeStruct(dims, dtype)


LINE = ("zh", "x", "core", "zl")


def line_pairs(k):
    pairs = []
    for zh in range(2):
        for x in range(4):
            for core in range(2):
                for zl in range(4):
                    z = 2 * ((zl + k + 2 * core) % 4) + (zh + x) % 2
                    to = ((z // 4 * 4 + x) * 2 + core) * 4 + z % 4
                    pairs.append((((zh * 4 + x) * 2 + core) * 4 + zl, to))
    return pairs


def row_block(k, core):
    step = 2 * lax.axis_index("zh") + lax.axis_index("zl") // 2
    return (step + 4 - k + 2 * core) % 4


NEXT = [(0, 1), (1, 0), (2, 3), (3, 2)]
SWAP = [(0, 1), (1, 0)]


def peer(slot, core):
    return (slot // 4 + 2 * core) % 4, (slot + 2 * core) % 4


def exchange(chunks):
    groups = []
    for zh in range(2):
        for core in range(2):
            for zl in range(4):
                peers = [peer(slot, core) for slot in range(16)]
                groups.append(
                    [(((y * 2 + zh) * 4 + x) * 2 + core) * 4 + zl for y, x in peers]
                )
    return lax.all_to_all(
        chunks, AXES, split_axis=0, concat_axis=0, tiled=True, axis_index_groups=groups
    )


def inverse(pairs):
    return [(b, a) for a, b in pairs]


def pieces(value):
    high = value.astype(BF16)
    rest = value - high.astype(F32)
    middle = rest.astype(BF16)
    low = (rest - middle.astype(F32)).astype(BF16)
    return [high.astype(F32), middle.astype(F32), low.astype(F32)]


def in_hbm(array):
    return pltpu.with_memory_space_constraint(array, pltpu.HBM)


def stat_rows(rows):
    pad = jnp.zeros((STAT - 6, ROWS), F32)
    return jnp.concatenate(rows + [pad], axis=0).astype(BF16)


def message_kernel(*refs):
    message, scratch, sem = refs[4], refs[5:9], refs[9]
    copies = [
        pltpu.make_async_copy(refs[i], scratch[i], sem.at[i]) for i in range(4)
    ]
    for copy in copies:
        copy.start()
    for copy in copies:
        copy.wait()
    queries, outputs, cotangent, log_norms = scratch
    sums = jnp.sum(
        cotangent[...].astype(F32) * outputs[...].astype(F32), axis=0, keepdims=True
    )
    zh, x, y = lax.axis_index("zh"), lax.axis_index("x"), lax.axis_index("y")
    head = 4 * y + 2 * zh + x // 2
    mine = lax.broadcasted_iota(jnp.int32, (HEADS, ROWS), 0) == head
    norms = jnp.sum(jnp.where(mine, log_norms[...], 0.0), axis=0, keepdims=True)
    message[:PART, :] = queries[...]
    message[PART : 2 * PART, :] = cotangent[...]
    message[2 * PART :, :] = stat_rows(pieces(sums) + pieces(norms))


def make_message(*args):
    return call(
        message_kernel,
        shape(2 * PART + STAT, ROWS),
        [HBM] * 4,
        VMEM,
        4,
        "message",
        [pltpu.VMEM(a.shape, a.dtype) for a in args] + [pltpu.SemaphoreType.DMA((4,))],
    )(*map(in_hbm, args))


def bundle_kernel(own, other, out):
    odd = lax.rem(lax.axis_index("x"), 2)
    for ref, place in ((own, odd), (other, 1 - odd)):
        start = pl.multiple_of(place * PART, PART)
        out[pl.ds(start, PART), :] = ref[:PART, :]
        out[pl.ds(start + 2 * PART, PART), :] = ref[PART : 2 * PART, :]
    one, two = own[2 * PART :, :].astype(F32), other[2 * PART :, :].astype(F32)
    both = one + two
    rows = pieces(both[0:1] + both[1:2] + both[2:3])
    out[4 * PART :, :] = stat_rows(rows + [one[3:6]])


def bundle(*args):
    return call(
        bundle_kernel, shape(4 * PART + STAT, ROWS), [VMEM] * 2, VMEM, 4, "bundle"
    )(*args)


def slot_columns(s):
    y, x = peer(s, lax.axis_index("core"))
    zh = (lax.axis_index("zl") + x) % 2
    return pl.ds(pl.multiple_of((4 * y + 2 * zh + x // 2) * DH, DH), DH)


def split_kernel(keys, values, out, held, in_sem, out_sem):
    pieces = [(s, a) for s in range(16) for a in range(2)]
    reads, writes = [], []
    for s, a in pieces:
        array = (keys, values)[a]
        at = held.at[s, a]
        number = 2 * s + a
        reads.append(
            pltpu.make_async_copy(array.at[:, slot_columns(s)], at, in_sem.at[number])
        )
        writes.append(pltpu.make_async_copy(at, out.at[s, a], out_sem.at[number]))
    for copy in reads:
        copy.start()
    for read, write in zip(reads, writes):
        read.wait()
        write.start()
    for copy in writes:
        copy.wait()


def split(keys, values):
    return call(
        split_kernel,
        pltpu.HBM((16, 2, KEYS, DH), BF16),
        [HBM] * 2,
        HBM,
        8,
        "split",
        [
            pltpu.VMEM((16, 2, KEYS, DH), BF16),
            pltpu.SemaphoreType.DMA((32,)),
            pltpu.SemaphoreType.DMA((32,)),
        ],
        pl.CostEstimate(flops=0, bytes_accessed=8 * MIB, transcendentals=0),
    )(in_hbm(keys), in_hbm(values))


def join_kernel(chunks, own, other, keys, values, queries):
    queries[...] = (own[...] + other[...].astype(F32)).astype(BF16)
    for s in range(16):
        columns = slot_columns(s)
        keys[:, columns] = chunks[s, 0]
        values[:, columns] = chunks[s, 1]


def join(chunks, own, other):
    out = shape(KEYS, HEADS * DH)
    outs = [out, out, shape(PART, ROWS)]
    return call(join_kernel, outs, [VMEM] * 3, [VMEM] * 3, 8, "join")(
        chunks, own, other
    )


def dot(a, b, ca, cb):
    return lax.dot_general(a, b, (((ca,), (cb,)), ((), ())), preferred_element_type=F32)


def assemble_kernel(*refs):
    mine, theirs, (qt, out, stat, dt, sem) = refs[:4], refs[4:8], refs[8:]
    core = lax.axis_index("core")
    for k in range(4):
        for ref, c in ((mine[k], core), (theirs[(k + 2) % 4], 1 - core)):
            zl = row_block(k, core)
            for xl in range(2):
                to = pl.ds(pl.multiple_of((2 * xl + c) * PART, PART), PART)
                qt[zl, to, :] = ref[xl * PART : (xl + 1) * PART, :]
                dt[zl, to, :] = ref[(2 + xl) * PART : (3 + xl) * PART, :]
        one = mine[k][4 * PART :, :].astype(F32)
        both = one + theirs[(k + 2) % 4][4 * PART :, :].astype(F32)
        stat[zl, 0:1, :] = both[0:1] + both[1:2] + both[2:3]
        stat[zl, 1:2, :] = (one[3:4] + one[4:5] + one[5:6]) * LOG2E
    copy = pltpu.make_async_copy(dt, out, sem)
    copy.start()
    copy.wait()


def assemble(mine, theirs):
    block = (4, DH, ROWS)
    return call(
        assemble_kernel,
        [shape(*block), pltpu.HBM(block, BF16), shape(4, 8, ROWS, dtype=F32)],
        [VMEM] * 8,
        [VMEM, HBM, VMEM],
        8,
        "assemble",
        [pltpu.VMEM(block, BF16), pltpu.SemaphoreType.DMA],
    )(*mine, *theirs)


def attention_kernel(
    qt, cotangent, stat, kv, grads, own, other, dt, dkv, dq, ds, sem, in_sem
):
    core = lax.axis_index("core")
    read = pltpu.make_async_copy(cotangent, dt, in_sem)
    read.start()
    read.wait()
    writes = []
    for block in range(8):
        rows = slice(block * 2 * KEYS, (block + 1) * 2 * KEYS)
        keys = kv[2 * block : 2 * block + 2, 0].reshape(2 * KEYS, DH)
        values = kv[2 * block : 2 * block + 2, 1].reshape(2 * KEYS, DH)
        weights, slopes = [], []
        for zl in range(4):
            score = dot(keys, qt[zl], 1, 0)
            weight = jnp.exp2(score * (FACTOR * LOG2E) - stat[zl, 1:2, :])
            slope = dot(values, dt[zl], 1, 0)
            grad = (weight * (slope - stat[zl, 0:1, :])).astype(BF16)
            weights.append(weight.astype(BF16))
            slopes.append(grad)
            ds[zl, rows, :] = grad
        value_grad = sum(dot(weights[zl], dt[zl], 1, 1) for zl in range(4))
        key_grad = sum(dot(slopes[zl], qt[zl], 1, 1) for zl in range(4)) * FACTOR
        for half in range(2):
            part = slice(half * KEYS, (half + 1) * KEYS)
            dkv[2 * block + half, 0] = key_grad[part].astype(BF16)
            dkv[2 * block + half, 1] = value_grad[part].astype(BF16)
        pair = slice(2 * block, 2 * block + 2)
        copy = pltpu.make_async_copy(dkv.at[pair], grads.at[pair], sem.at[block])
        copy.start()
        writes.append(copy)
    keys = kv[:, 0].reshape(16 * KEYS, DH)
    for zl in range(4):
        dq[zl] = dot(keys, ds[zl], 0, 0) * FACTOR
    for k in range(4):
        zl = row_block(k, core)
        for xl in range(2):
            at = pl.ds(pl.multiple_of((2 * xl + core) * PART, PART), PART)
            own[k, xl] = dq[zl, at, :]
            at = pl.ds(pl.multiple_of((2 * xl + 1 - core) * PART, PART), PART)
            other[(k + 2) % 4, xl] = dq[zl, at, :].astype(BF16)
    for copy in writes:
        copy.wait()


def attention(qt, dt, stat, kv):
    part = (4, 2, PART, ROWS)
    return call(
        attention_kernel,
        [pltpu.HBM((16, 2, KEYS, DH), BF16), shape(*part, dtype=F32), shape(*part)],
        [VMEM, HBM, VMEM, VMEM],
        [HBM, VMEM, VMEM],
        32,
        "attention",
        [
            pltpu.VMEM((4, DH, ROWS), BF16),
            pltpu.VMEM((16, 2, KEYS, DH), BF16),
            pltpu.VMEM((4, DH, ROWS), F32),
            pltpu.VMEM((4, 16 * KEYS, ROWS), BF16),
            pltpu.SemaphoreType.DMA((8,)),
            pltpu.SemaphoreType.DMA,
        ],
        pl.CostEstimate(
            flops=5 * 2 * 2048 * 1024 * 256,
            bytes_accessed=8 * MIB,
            transcendentals=2048 * 1024,
        ),
    )(qt, in_hbm(dt), stat, kv)


def core_sum_kernel(own, other, *outs):
    for d, out in enumerate(outs):
        out[...] = (own[d] + other[d].astype(F32)).astype(BF16)


def core_sum(own, other):
    return call(
        core_sum_kernel,
        [shape(2, PART, ROWS)] * 4,
        [VMEM] * 2,
        [VMEM] * 4,
        4,
        "core_sum",
    )(own, other)


def line_sum_kernel(*refs):
    parts, own, other = refs[:4], refs[4], refs[5]
    odd = lax.rem(lax.axis_index("x"), 2)
    for out, place in ((own, odd), (other, 1 - odd)):
        total = parts[0][place].astype(F32)
        for part in parts[1:]:
            total = total + part[place].astype(F32)
        out[...] = total.astype(out.dtype)


def line_sum(parts):
    outs = [shape(PART, ROWS, dtype=F32), shape(PART, ROWS)]
    return call(line_sum_kernel, outs, [VMEM] * 4, [VMEM] * 2, 4, "line_sum")(*parts)


def local(queries, outputs, cotangent, log_norms, memory_keys, memory_values):
    message = make_message(queries.T, outputs.T, cotangent.T, log_norms.T)
    other = lax.ppermute(message, "x", NEXT)
    chunks = split(memory_keys, memory_values)
    chunks, other = lax.optimization_barrier((chunks, other))
    received = exchange(chunks)
    part = bundle(message, other)
    mine = [lax.ppermute(part, LINE, line_pairs(k)) for k in range(4)]
    theirs = [lax.ppermute(part, "core", SWAP) for part in mine]
    grads, own, other = attention(*assemble(mine, theirs), received)
    returned = exchange(grads)
    sums = core_sum(own, lax.ppermute(other, "core", SWAP))
    sums = [lax.ppermute(sums[k], LINE, inverse(line_pairs(k))) for k in range(4)]
    own, other = line_sum(sums)
    other = lax.ppermute(other, "x", NEXT)
    key_grads, value_grads, query_grads = join(returned, own, other)
    return query_grads.T, key_grads, value_grads


def solution(mesh):
    fine = Mesh(mesh.devices.reshape(SIZES), AXES)
    return jax.shard_map(
        local,
        mesh=fine,
        in_specs=(
            P("zl", MEM),
            P("zl", MEM),
            P("zl", MEM),
            P("zl", None),
            P(MEM + ("zl",), None),
            P(MEM + ("zl",), None),
        ),
        out_specs=(P("zl", MEM), P(MEM + ("zl",), None), P(MEM + ("zl",), None)),
        check_vma=False,
    )
```

```python
import jax
import jax.numpy as jnp
from jax import lax
from jax.experimental import pallas as pl
from jax.experimental.pallas import tpu as pltpu
from jax.sharding import Mesh, PartitionSpec as P

AXES = ("y", "zh", "x", "core", "zl")
SIZES = (4, 2, 4, 2, 4)
MEM = ("y", "zh", "x", "core")
HEADS = 16
DH = 256
ROWS = 256
PART = 64
KEYS = 128
STAT = 16
FACTOR = DH**-0.5
LOG2E = 1.4426950408889634
MIB = 1024 * 1024
BF16, F32 = jnp.bfloat16, jnp.float32
HBM = pl.BlockSpec(memory_space=pltpu.HBM)
VMEM = pl.BlockSpec(memory_space=pltpu.VMEM)


def call(kernel, outs, ins, out_specs, limit, name, scratch=(), cost=None):
    return pl.pallas_call(
        kernel,
        out_shape=outs,
        in_specs=ins,
        out_specs=out_specs,
        scratch_shapes=list(scratch),
        compiler_params=pltpu.CompilerParams(vmem_limit_bytes=limit * MIB),
        cost_estimate=cost,
        name=name,
    )


def shape(*dims, dtype=BF16):
    return jax.ShapeDtypeStruct(dims, dtype)


LINE = ("zh", "x", "zl")
MIRROR = [
    ((zh * 4 + x) * 4 + zl, ((1 - zh) * 4 + x) * 4 + 3 - zl)
    for zh in range(2)
    for x in (1, 3)
    for zl in range(4)
]


def turn(k):
    return [(i, i ^ k) for i in range(4)]


NEXT = [(0, 1), (1, 0), (2, 3), (3, 2)]
SWAP = [(0, 1), (1, 0)]


def peer(slot, core):
    return (slot // 4 + 2 * core) % 4, (slot + 2 * core) % 4


def exchange(chunks):
    groups = []
    for zh in range(2):
        for core in range(2):
            for zl in range(4):
                peers = [peer(slot, core) for slot in range(16)]
                groups.append(
                    [(((y * 2 + zh) * 4 + x) * 2 + core) * 4 + zl for y, x in peers]
                )
    return lax.all_to_all(
        chunks, AXES, split_axis=0, concat_axis=0, tiled=True, axis_index_groups=groups
    )


def pieces(value):
    high = value.astype(BF16)
    rest = value - high.astype(F32)
    middle = rest.astype(BF16)
    low = (rest - middle.astype(F32)).astype(BF16)
    return [high.astype(F32), middle.astype(F32), low.astype(F32)]


def in_hbm(array):
    return pltpu.with_memory_space_constraint(array, pltpu.HBM)


def stat_rows(rows):
    pad = jnp.zeros((STAT - 6, ROWS), F32)
    return jnp.concatenate(rows + [pad], axis=0).astype(BF16)


def message_kernel(*refs):
    message, scratch, sem = refs[4], refs[5:9], refs[9]
    copies = [
        pltpu.make_async_copy(refs[i], scratch[i], sem.at[i]) for i in range(4)
    ]
    for copy in copies:
        copy.start()
    for copy in copies:
        copy.wait()
    queries, outputs, cotangent, log_norms = scratch
    sums = jnp.sum(
        cotangent[...].astype(F32) * outputs[...].astype(F32), axis=0, keepdims=True
    )
    zh, x, y = lax.axis_index("zh"), lax.axis_index("x"), lax.axis_index("y")
    head = 4 * y + 2 * zh + x // 2
    mine = lax.broadcasted_iota(jnp.int32, (HEADS, ROWS), 0) == head
    norms = jnp.sum(jnp.where(mine, log_norms[...], 0.0), axis=0, keepdims=True)
    message[:PART, :] = queries[...]
    message[PART : 2 * PART, :] = cotangent[...]
    message[2 * PART :, :] = stat_rows(pieces(sums) + pieces(norms))


def make_message(*args):
    return call(
        message_kernel,
        shape(2 * PART + STAT, ROWS),
        [HBM] * 4,
        VMEM,
        4,
        "message",
        [pltpu.VMEM(a.shape, a.dtype) for a in args] + [pltpu.SemaphoreType.DMA((4,))],
    )(*map(in_hbm, args))


def bundle_kernel(own, other, out):
    odd = lax.rem(lax.axis_index("x"), 2)
    for ref, place in ((own, odd), (other, 1 - odd)):
        start = pl.multiple_of(place * PART, PART)
        out[pl.ds(start, PART), :] = ref[:PART, :]
        out[pl.ds(start + 2 * PART, PART), :] = ref[PART : 2 * PART, :]
    one, two = own[2 * PART :, :].astype(F32), other[2 * PART :, :].astype(F32)
    both = one + two
    rows = pieces(both[0:1] + both[1:2] + both[2:3])
    out[4 * PART :, :] = stat_rows(rows + [one[3:6]])


def bundle(*args):
    return call(
        bundle_kernel, shape(4 * PART + STAT, ROWS), [VMEM] * 2, VMEM, 4, "bundle"
    )(*args)


def slot_columns(s):
    y, x = peer(s, lax.axis_index("core"))
    zh = (lax.axis_index("zh") + x) % 2
    return pl.ds(pl.multiple_of((4 * y + 2 * zh + x // 2) * DH, DH), DH)


def split_kernel(keys, values, out, held, in_sem, out_sem):
    pieces = [(s, a) for s in range(16) for a in range(2)]
    reads, writes = [], []
    for s, a in pieces:
        array = (keys, values)[a]
        at = held.at[s, a]
        number = 2 * s + a
        reads.append(
            pltpu.make_async_copy(array.at[:, slot_columns(s)], at, in_sem.at[number])
        )
        writes.append(pltpu.make_async_copy(at, out.at[s, a], out_sem.at[number]))
    for copy in reads:
        copy.start()
    for read, write in zip(reads, writes):
        read.wait()
        write.start()
    for copy in writes:
        copy.wait()


def split(keys, values):
    return call(
        split_kernel,
        pltpu.HBM((16, 2, KEYS, DH), BF16),
        [HBM] * 2,
        HBM,
        8,
        "split",
        [
            pltpu.VMEM((16, 2, KEYS, DH), BF16),
            pltpu.SemaphoreType.DMA((32,)),
            pltpu.SemaphoreType.DMA((32,)),
        ],
        pl.CostEstimate(flops=0, bytes_accessed=8 * MIB, transcendentals=0),
    )(in_hbm(keys), in_hbm(values))


def join_kernel(chunks, own, other, keys, values, queries):
    queries[...] = (own[...].astype(F32) + other[...].astype(F32)).astype(BF16)
    for s in range(16):
        columns = slot_columns(s)
        keys[:, columns] = chunks[s, 0]
        values[:, columns] = chunks[s, 1]


def join(chunks, own, other):
    out = shape(KEYS, HEADS * DH)
    outs = [out, out, shape(PART, ROWS)]
    return call(join_kernel, outs, [VMEM] * 3, [VMEM] * 3, 8, "join")(
        chunks, own, other
    )


def dot(a, b, ca, cb):
    return lax.dot_general(a, b, (((ca,), (cb,)), ((), ())), preferred_element_type=F32)


def assemble_kernel(*refs):
    mine, theirs, (qt, out, stat, dt, sem) = refs[:4], refs[4:8], refs[8:]
    core = lax.axis_index("core")
    for k in range(4):
        zl = k
        for ref, c in ((mine[k], core), (theirs[k], 1 - core)):
            for xl in range(2):
                to = pl.ds(pl.multiple_of((2 * xl + c) * PART, PART), PART)
                qt[zl, to, :] = ref[xl * PART : (xl + 1) * PART, :]
                dt[zl, to, :] = ref[(2 + xl) * PART : (3 + xl) * PART, :]
        one = mine[k][4 * PART :, :].astype(F32)
        both = one + theirs[k][4 * PART :, :].astype(F32)
        stat[zl, 0:1, :] = both[0:1] + both[1:2] + both[2:3]
        stat[zl, 1:2, :] = (one[3:4] + one[4:5] + one[5:6]) * LOG2E
    copy = pltpu.make_async_copy(dt, out, sem)
    copy.start()
    copy.wait()


def assemble(mine, theirs):
    block = (4, DH, ROWS)
    return call(
        assemble_kernel,
        [shape(*block), pltpu.HBM(block, BF16), shape(4, 8, ROWS, dtype=F32)],
        [VMEM] * 8,
        [VMEM, HBM, VMEM],
        8,
        "assemble",
        [pltpu.VMEM(block, BF16), pltpu.SemaphoreType.DMA],
    )(*mine, *theirs)


def attention_kernel(
    qt, cotangent, stat, kv, grads, own, other, dt, dkv, dq, ds, sem, in_sem
):
    core = lax.axis_index("core")
    read = pltpu.make_async_copy(cotangent, dt, in_sem)
    read.start()
    read.wait()
    writes = []
    for block in range(8):
        rows = slice(block * 2 * KEYS, (block + 1) * 2 * KEYS)
        keys = kv[2 * block : 2 * block + 2, 0].reshape(2 * KEYS, DH)
        values = kv[2 * block : 2 * block + 2, 1].reshape(2 * KEYS, DH)
        weights, slopes = [], []
        for zl in range(4):
            score = dot(keys, qt[zl], 1, 0)
            weight = jnp.exp2(score * (FACTOR * LOG2E) - stat[zl, 1:2, :])
            slope = dot(values, dt[zl], 1, 0)
            grad = (weight * (slope - stat[zl, 0:1, :])).astype(BF16)
            weights.append(weight.astype(BF16))
            slopes.append(grad)
            ds[zl, rows, :] = grad
        value_grad = sum(dot(weights[zl], dt[zl], 1, 1) for zl in range(4))
        key_grad = sum(dot(slopes[zl], qt[zl], 1, 1) for zl in range(4)) * FACTOR
        for half in range(2):
            part = slice(half * KEYS, (half + 1) * KEYS)
            dkv[2 * block + half, 0] = key_grad[part].astype(BF16)
            dkv[2 * block + half, 1] = value_grad[part].astype(BF16)
        pair = slice(2 * block, 2 * block + 2)
        copy = pltpu.make_async_copy(dkv.at[pair], grads.at[pair], sem.at[block])
        copy.start()
        writes.append(copy)
    keys = kv[:, 0].reshape(16 * KEYS, DH)
    for zl in range(4):
        dq[zl] = dot(keys, ds[zl], 0, 0) * FACTOR
    for k in range(4):
        zl = k
        for xl in range(2):
            at = pl.ds(pl.multiple_of((2 * xl + core) * PART, PART), PART)
            own[k, xl] = dq[zl, at, :]
            at = pl.ds(pl.multiple_of((2 * xl + 1 - core) * PART, PART), PART)
            other[k, xl] = dq[zl, at, :].astype(BF16)
    for copy in writes:
        copy.wait()


def attention(qt, dt, stat, kv):
    part = (4, 2, PART, ROWS)
    return call(
        attention_kernel,
        [pltpu.HBM((16, 2, KEYS, DH), BF16), shape(*part, dtype=F32), shape(*part)],
        [VMEM, HBM, VMEM, VMEM],
        [HBM, VMEM, VMEM],
        32,
        "attention",
        [
            pltpu.VMEM((4, DH, ROWS), BF16),
            pltpu.VMEM((16, 2, KEYS, DH), BF16),
            pltpu.VMEM((4, DH, ROWS), F32),
            pltpu.VMEM((4, 16 * KEYS, ROWS), BF16),
            pltpu.SemaphoreType.DMA((8,)),
            pltpu.SemaphoreType.DMA,
        ],
        pl.CostEstimate(
            flops=5 * 2 * 2048 * 1024 * 256,
            bytes_accessed=8 * MIB,
            transcendentals=2048 * 1024,
        ),
    )(qt, in_hbm(dt), stat, kv)


def core_sum_kernel(own, other, *outs):
    for d, out in enumerate(outs):
        out[...] = (own[d] + other[d].astype(F32)).astype(BF16)


def core_sum(own, other):
    return call(
        core_sum_kernel,
        [shape(2, PART, ROWS)] * 4,
        [VMEM] * 2,
        [VMEM] * 4,
        4,
        "core_sum",
    )(own, other)


def line_sum_kernel(*refs):
    total = refs[0][...].astype(F32)
    for part in refs[1:4]:
        total = total + part[...].astype(F32)
    refs[4][...] = total.astype(BF16)


def line_sum(parts):
    out = shape(2, PART, ROWS)
    return call(line_sum_kernel, out, [VMEM] * 4, VMEM, 4, "line_sum")(*parts)


def pick_kernel(kept, crossed, own, other):
    odd = lax.rem(lax.axis_index("x"), 2)

    @pl.when(odd == 0)
    def _():
        own[...] = kept[0]
        other[...] = kept[1]

    @pl.when(odd == 1)
    def _():
        own[...] = crossed[1]
        other[...] = crossed[0]


def pick(kept, crossed):
    outs = [shape(PART, ROWS)] * 2
    return call(pick_kernel, outs, [VMEM] * 2, [VMEM] * 2, 4, "pick")(kept, crossed)


def choose_kernel(kept, crossed, out):
    odd = lax.rem(lax.axis_index("x"), 2)

    @pl.when(odd == 0)
    def _():
        out[...] = kept[...]

    @pl.when(odd == 1)
    def _():
        out[...] = crossed[...]


def choose(kept, crossed):
    out = shape(*kept.shape)
    return call(choose_kernel, out, [VMEM] * 2, VMEM, 4, "choose")(kept, crossed)


def local(queries, outputs, cotangent, log_norms, memory_keys, memory_values):
    message = make_message(queries.T, outputs.T, cotangent.T, log_norms.T)
    other = lax.ppermute(message, "x", NEXT)
    chunks = split(memory_keys, memory_values)
    chunks, other = lax.optimization_barrier((chunks, other))
    received = exchange(chunks)
    part = bundle(message, other)
    part = choose(part, lax.ppermute(part, LINE, MIRROR))
    mine = [part] + [lax.ppermute(part, "zl", turn(k)) for k in (1, 2, 3)]
    theirs = [lax.ppermute(part, "core", SWAP) for part in mine]
    grads, own, other = attention(*assemble(mine, theirs), received)
    returned = exchange(grads)
    sums = core_sum(own, lax.ppermute(other, "core", SWAP))
    sums = [sums[0]] + [lax.ppermute(sums[k], "zl", turn(k)) for k in (1, 2, 3)]
    total = line_sum(sums)
    own, other = pick(total, lax.ppermute(total, LINE, MIRROR))
    other = lax.ppermute(other, "x", NEXT)
    key_grads, value_grads, query_grads = join(returned, own, other)
    return query_grads.T, key_grads, value_grads


def solution(mesh):
    fine = Mesh(mesh.devices.reshape(SIZES), AXES)
    return jax.shard_map(
        local,
        mesh=fine,
        in_specs=(
            P("zl", MEM),
            P("zl", MEM),
            P("zl", MEM),
            P("zl", None),
            P(MEM + ("zl",), None),
            P(MEM + ("zl",), None),
        ),
        out_specs=(P("zl", MEM), P(MEM + ("zl",), None), P(MEM + ("zl",), None)),
        check_vma=False,
    )
```

```python
import jax
import jax.numpy as jnp
from jax import lax
from jax.experimental import pallas as pl
from jax.experimental.pallas import tpu as pltpu
from jax.sharding import Mesh, PartitionSpec as P

AXES = ("y", "zh", "x", "core", "zl")
SIZES = (4, 2, 4, 2, 4)
MEM = ("y", "zh", "x", "core")
HEADS = 16
DH = 256
ROWS = 256
PART = 64
KEYS = 128
STAT = 16
FACTOR = DH**-0.5
LOG2E = 1.4426950408889634
MIB = 1024 * 1024
BF16, F32 = jnp.bfloat16, jnp.float32
HBM = pl.BlockSpec(memory_space=pltpu.HBM)
VMEM = pl.BlockSpec(memory_space=pltpu.VMEM)


def call(kernel, outs, ins, out_specs, limit, name, scratch=(), cost=None):
    return pl.pallas_call(
        kernel,
        out_shape=outs,
        in_specs=ins,
        out_specs=out_specs,
        scratch_shapes=list(scratch),
        compiler_params=pltpu.CompilerParams(vmem_limit_bytes=limit * MIB),
        cost_estimate=cost,
        name=name,
    )


def shape(*dims, dtype=BF16):
    return jax.ShapeDtypeStruct(dims, dtype)


LINE = ("zh", "x", "zl")
MIRROR = [
    ((zh * 4 + x) * 4 + zl, ((1 - zh) * 4 + x) * 4 + 3 - zl)
    for zh in range(2)
    for x in (1, 3)
    for zl in range(4)
]


def turn(k):
    return [(i, i ^ k) for i in range(4)]


NEXT = [(0, 1), (1, 0), (2, 3), (3, 2)]
SWAP = [(0, 1), (1, 0)]


def peer(slot, core):
    return (slot // 4 + 2 * core) % 4, (slot + 2 * core) % 4


def exchange(chunks):
    groups = []
    for zh in range(2):
        for core in range(2):
            for zl in range(4):
                peers = [peer(slot, core) for slot in range(16)]
                groups.append(
                    [(((y * 2 + zh) * 4 + x) * 2 + core) * 4 + zl for y, x in peers]
                )
    return lax.all_to_all(
        chunks, AXES, split_axis=0, concat_axis=0, tiled=True, axis_index_groups=groups
    )


def pieces(value):
    high = value.astype(BF16)
    rest = value - high.astype(F32)
    middle = rest.astype(BF16)
    low = (rest - middle.astype(F32)).astype(BF16)
    return [high.astype(F32), middle.astype(F32), low.astype(F32)]


def in_hbm(array):
    return pltpu.with_memory_space_constraint(array, pltpu.HBM)


def stat_rows(rows):
    pad = jnp.zeros((STAT - 6, ROWS), F32)
    return jnp.concatenate(rows + [pad], axis=0).astype(BF16)


def message_kernel(*refs):
    message, scratch, sem = refs[4], refs[5:9], refs[9]
    copies = [
        pltpu.make_async_copy(refs[i], scratch[i], sem.at[i]) for i in range(4)
    ]
    for copy in copies:
        copy.start()
    for copy in copies:
        copy.wait()
    queries, outputs, cotangent, log_norms = scratch
    sums = jnp.sum(
        cotangent[...].astype(F32) * outputs[...].astype(F32), axis=0, keepdims=True
    )
    zh, x, y = lax.axis_index("zh"), lax.axis_index("x"), lax.axis_index("y")
    head = 4 * y + 2 * zh + x // 2
    mine = lax.broadcasted_iota(jnp.int32, (HEADS, ROWS), 0) == head
    norms = jnp.sum(jnp.where(mine, log_norms[...], 0.0), axis=0, keepdims=True)
    message[:PART, :] = queries[...]
    message[PART : 2 * PART, :] = cotangent[...]
    message[2 * PART :, :] = stat_rows(pieces(sums) + pieces(norms))


def make_message(*args):
    return call(
        message_kernel,
        shape(2 * PART + STAT, ROWS),
        [HBM] * 4,
        VMEM,
        4,
        "message",
        [pltpu.VMEM(a.shape, a.dtype) for a in args] + [pltpu.SemaphoreType.DMA((4,))],
    )(*map(in_hbm, args))


def bundle_kernel(own, other, out):
    odd = lax.rem(lax.axis_index("x"), 2)
    for ref, place in ((own, odd), (other, 1 - odd)):
        start = pl.multiple_of(place * PART, PART)
        out[pl.ds(start, PART), :] = ref[:PART, :]
        out[pl.ds(start + 2 * PART, PART), :] = ref[PART : 2 * PART, :]
    one, two = own[2 * PART :, :].astype(F32), other[2 * PART :, :].astype(F32)
    both = one + two
    rows = pieces(both[0:1] + both[1:2] + both[2:3])
    out[4 * PART :, :] = stat_rows(rows + [one[3:6]])


def bundle(*args):
    return call(
        bundle_kernel, shape(4 * PART + STAT, ROWS), [VMEM] * 2, VMEM, 4, "bundle"
    )(*args)


def slot_columns(s):
    y, x = peer(s, lax.axis_index("core"))
    zh = (lax.axis_index("zh") + x) % 2
    return pl.ds(pl.multiple_of((4 * y + 2 * zh + x // 2) * DH, DH), DH)


def split_kernel(keys, values, out, held, in_sem, out_sem):
    pieces = [(s, a) for s in range(16) for a in range(2)]
    reads, writes = [], []
    for s, a in pieces:
        array = (keys, values)[a]
        at = held.at[s, a]
        number = 2 * s + a
        reads.append(
            pltpu.make_async_copy(array.at[:, slot_columns(s)], at, in_sem.at[number])
        )
        writes.append(pltpu.make_async_copy(at, out.at[s, a], out_sem.at[number]))
    for copy in reads:
        copy.start()
    for read, write in zip(reads, writes):
        read.wait()
        write.start()
    for copy in writes:
        copy.wait()


def split(keys, values):
    return call(
        split_kernel,
        pltpu.HBM((16, 2, KEYS, DH), BF16),
        [HBM] * 2,
        HBM,
        8,
        "split",
        [
            pltpu.VMEM((16, 2, KEYS, DH), BF16),
            pltpu.SemaphoreType.DMA((32,)),
            pltpu.SemaphoreType.DMA((32,)),
        ],
        pl.CostEstimate(flops=0, bytes_accessed=8 * MIB, transcendentals=0),
    )(in_hbm(keys), in_hbm(values))


def join_kernel(chunks, own, other, keys, values, queries):
    queries[...] = (own[...].astype(F32) + other[...].astype(F32)).astype(BF16)
    for s in range(16):
        columns = slot_columns(s)
        keys[:, columns] = chunks[s, 0]
        values[:, columns] = chunks[s, 1]


def join(chunks, own, other):
    out = shape(KEYS, HEADS * DH)
    outs = [out, out, shape(PART, ROWS)]
    return call(join_kernel, outs, [VMEM] * 3, [VMEM] * 3, 8, "join")(
        chunks, own, other
    )


def dot(a, b, ca, cb):
    return lax.dot_general(a, b, (((ca,), (cb,)), ((), ())), preferred_element_type=F32)


def assemble_kernel(*refs):
    mine, theirs, (qt, out, stat, dt, sem) = refs[:4], refs[4:8], refs[8:]
    core = lax.axis_index("core")
    for k in range(4):
        zl = k
        for ref, c in ((mine[k], core), (theirs[k], 1 - core)):
            for xl in range(2):
                to = pl.ds(pl.multiple_of((2 * xl + c) * PART, PART), PART)
                qt[zl, to, :] = ref[xl * PART : (xl + 1) * PART, :]
                dt[zl, to, :] = ref[(2 + xl) * PART : (3 + xl) * PART, :]
        one = mine[k][4 * PART :, :].astype(F32)
        both = one + theirs[k][4 * PART :, :].astype(F32)
        stat[zl, 0:1, :] = both[0:1] + both[1:2] + both[2:3]
        stat[zl, 1:2, :] = (one[3:4] + one[4:5] + one[5:6]) * LOG2E
    copy = pltpu.make_async_copy(dt, out, sem)
    copy.start()
    copy.wait()


def assemble(mine, theirs):
    block = (4, DH, ROWS)
    return call(
        assemble_kernel,
        [shape(*block), pltpu.HBM(block, BF16), shape(4, 8, ROWS, dtype=F32)],
        [VMEM] * 8,
        [VMEM, HBM, VMEM],
        8,
        "assemble",
        [pltpu.VMEM(block, BF16), pltpu.SemaphoreType.DMA],
    )(*mine, *theirs)


def attention_kernel(
    qt, cotangent, stat, kv, grads, own, other, dt, dkv, dq, ds, sem, in_sem
):
    core = lax.axis_index("core")
    read = pltpu.make_async_copy(cotangent, dt, in_sem)
    read.start()
    read.wait()
    writes = []
    for block in range(4):
        rows = slice(block * 4 * KEYS, (block + 1) * 4 * KEYS)
        keys = kv[4 * block : 4 * block + 4, 0].reshape(4 * KEYS, DH)
        values = kv[4 * block : 4 * block + 4, 1].reshape(4 * KEYS, DH)
        weights, slopes = [], []
        for zl in range(4):
            score = dot(keys, qt[zl], 1, 0)
            weight = jnp.exp2(score * (FACTOR * LOG2E) - stat[zl, 1:2, :])
            slope = dot(values, dt[zl], 1, 0)
            grad = (weight * (slope - stat[zl, 0:1, :])).astype(BF16)
            weights.append(weight.astype(BF16))
            slopes.append(grad)
            ds[zl, rows, :] = grad
        value_grad = sum(dot(weights[zl], dt[zl], 1, 1) for zl in range(4))
        key_grad = sum(dot(slopes[zl], qt[zl], 1, 1) for zl in range(4)) * FACTOR
        for place in range(4):
            part = slice(place * KEYS, (place + 1) * KEYS)
            dkv[4 * block + place, 0] = key_grad[part].astype(BF16)
            dkv[4 * block + place, 1] = value_grad[part].astype(BF16)
        slots = slice(4 * block, 4 * block + 4)
        copy = pltpu.make_async_copy(dkv.at[slots], grads.at[slots], sem.at[block])
        copy.start()
        writes.append(copy)
    keys = kv[:, 0].reshape(16 * KEYS, DH)
    for zl in range(4):
        dq[zl] = dot(keys, ds[zl], 0, 0) * FACTOR
    for k in range(4):
        zl = k
        for xl in range(2):
            at = pl.ds(pl.multiple_of((2 * xl + core) * PART, PART), PART)
            own[k, xl] = dq[zl, at, :]
            at = pl.ds(pl.multiple_of((2 * xl + 1 - core) * PART, PART), PART)
            other[k, xl] = dq[zl, at, :].astype(BF16)
    for copy in writes:
        copy.wait()


def attention(qt, dt, stat, kv):
    part = (4, 2, PART, ROWS)
    return call(
        attention_kernel,
        [pltpu.HBM((16, 2, KEYS, DH), BF16), shape(*part, dtype=F32), shape(*part)],
        [VMEM, HBM, VMEM, VMEM],
        [HBM, VMEM, VMEM],
        32,
        "attention",
        [
            pltpu.VMEM((4, DH, ROWS), BF16),
            pltpu.VMEM((16, 2, KEYS, DH), BF16),
            pltpu.VMEM((4, DH, ROWS), F32),
            pltpu.VMEM((4, 16 * KEYS, ROWS), BF16),
            pltpu.SemaphoreType.DMA((8,)),
            pltpu.SemaphoreType.DMA,
        ],
        pl.CostEstimate(
            flops=5 * 2 * 2048 * 1024 * 256,
            bytes_accessed=8 * MIB,
            transcendentals=2048 * 1024,
        ),
    )(qt, in_hbm(dt), stat, kv)


def core_sum_kernel(own, other, *outs):
    for d, out in enumerate(outs):
        out[...] = (own[d] + other[d].astype(F32)).astype(BF16)


def core_sum(own, other):
    return call(
        core_sum_kernel,
        [shape(2, PART, ROWS)] * 4,
        [VMEM] * 2,
        [VMEM] * 4,
        4,
        "core_sum",
    )(own, other)


def line_sum_kernel(*refs):
    total = refs[0][...].astype(F32)
    for part in refs[1:4]:
        total = total + part[...].astype(F32)
    refs[4][...] = total.astype(BF16)


def line_sum(parts):
    out = shape(2, PART, ROWS)
    return call(line_sum_kernel, out, [VMEM] * 4, VMEM, 4, "line_sum")(*parts)


def pick_kernel(kept, crossed, own, other):
    odd = lax.rem(lax.axis_index("x"), 2)

    @pl.when(odd == 0)
    def _():
        own[...] = kept[0]
        other[...] = kept[1]

    @pl.when(odd == 1)
    def _():
        own[...] = crossed[1]
        other[...] = crossed[0]


def pick(kept, crossed):
    outs = [shape(PART, ROWS)] * 2
    return call(pick_kernel, outs, [VMEM] * 2, [VMEM] * 2, 4, "pick")(kept, crossed)


def choose_kernel(kept, crossed, out):
    odd = lax.rem(lax.axis_index("x"), 2)

    @pl.when(odd == 0)
    def _():
        out[...] = kept[...]

    @pl.when(odd == 1)
    def _():
        out[...] = crossed[...]


def choose(kept, crossed):
    out = shape(*kept.shape)
    return call(choose_kernel, out, [VMEM] * 2, VMEM, 4, "choose")(kept, crossed)


def local(queries, outputs, cotangent, log_norms, memory_keys, memory_values):
    message = make_message(queries.T, outputs.T, cotangent.T, log_norms.T)
    other = lax.ppermute(message, "x", NEXT)
    chunks = split(memory_keys, memory_values)
    chunks, other = lax.optimization_barrier((chunks, other))
    received = exchange(chunks)
    part = bundle(message, other)
    part = choose(part, lax.ppermute(part, LINE, MIRROR))
    mine = [part] + [lax.ppermute(part, "zl", turn(k)) for k in (1, 2, 3)]
    theirs = [lax.ppermute(part, "core", SWAP) for part in mine]
    grads, own, other = attention(*assemble(mine, theirs), received)
    returned = exchange(grads)
    sums = core_sum(own, lax.ppermute(other, "core", SWAP))
    sums = [sums[0]] + [lax.ppermute(sums[k], "zl", turn(k)) for k in (1, 2, 3)]
    total = line_sum(sums)
    own, other = pick(total, lax.ppermute(total, LINE, MIRROR))
    other = lax.ppermute(other, "x", NEXT)
    key_grads, value_grads, query_grads = join(returned, own, other)
    return query_grads.T, key_grads, value_grads


def solution(mesh):
    fine = Mesh(mesh.devices.reshape(SIZES), AXES)
    return jax.shard_map(
        local,
        mesh=fine,
        in_specs=(
            P("zl", MEM),
            P("zl", MEM),
            P("zl", MEM),
            P("zl", None),
            P(MEM + ("zl",), None),
            P(MEM + ("zl",), None),
        ),
        out_specs=(P("zl", MEM), P(MEM + ("zl",), None), P(MEM + ("zl",), None)),
        check_vma=False,
    )
```

```python
import jax
import jax.numpy as jnp
from jax import lax
from jax.experimental import pallas as pl
from jax.experimental.pallas import tpu as pltpu
from jax.sharding import Mesh, PartitionSpec as P

AXES = ("y", "zh", "x", "core", "zl")
SIZES = (4, 2, 4, 2, 4)
MEM = ("y", "zh", "x", "core")
HEADS = 16
DH = 256
ROWS = 256
PART = 64
KEYS = 128
STAT = 16
FACTOR = DH**-0.5
LOG2E = 1.4426950408889634
MIB = 1024 * 1024
BF16, F32 = jnp.bfloat16, jnp.float32
HBM = pl.BlockSpec(memory_space=pltpu.HBM)
VMEM = pl.BlockSpec(memory_space=pltpu.VMEM)


def call(kernel, outs, ins, out_specs, limit, name, scratch=(), cost=None):
    return pl.pallas_call(
        kernel,
        out_shape=outs,
        in_specs=ins,
        out_specs=out_specs,
        scratch_shapes=list(scratch),
        compiler_params=pltpu.CompilerParams(vmem_limit_bytes=limit * MIB),
        cost_estimate=cost,
        name=name,
    )


def shape(*dims, dtype=BF16):
    return jax.ShapeDtypeStruct(dims, dtype)


LINE = ("zh", "x", "zl")
MIRROR = [
    ((zh * 4 + x) * 4 + zl, ((1 - zh) * 4 + x) * 4 + 3 - zl)
    for zh in range(2)
    for x in (1, 3)
    for zl in range(4)
]


def turn(k):
    return [(i, i ^ k) for i in range(4)]


NEXT = [(0, 1), (1, 0), (2, 3), (3, 2)]
SWAP = [(0, 1), (1, 0)]


def peer(slot, core):
    return (slot // 4 + 2 * core) % 4, (slot + 2 * core) % 4


def exchange(chunks):
    groups = []
    for zh in range(2):
        for core in range(2):
            for zl in range(4):
                peers = [peer(slot, core) for slot in range(16)]
                groups.append(
                    [(((y * 2 + zh) * 4 + x) * 2 + core) * 4 + zl for y, x in peers]
                )
    return lax.all_to_all(
        chunks, AXES, split_axis=0, concat_axis=0, tiled=True, axis_index_groups=groups
    )


def pieces(value):
    high = value.astype(BF16)
    rest = value - high.astype(F32)
    middle = rest.astype(BF16)
    low = (rest - middle.astype(F32)).astype(BF16)
    return [high.astype(F32), middle.astype(F32), low.astype(F32)]


def in_hbm(array):
    return pltpu.with_memory_space_constraint(array, pltpu.HBM)


def stat_rows(rows):
    pad = jnp.zeros((STAT - 6, ROWS), F32)
    return jnp.concatenate(rows + [pad], axis=0).astype(BF16)


def message_kernel(*refs):
    message, scratch, sem = refs[4], refs[5:9], refs[9]
    copies = [
        pltpu.make_async_copy(refs[i], scratch[i], sem.at[i]) for i in range(4)
    ]
    for copy in copies:
        copy.start()
    for copy in copies:
        copy.wait()
    queries, outputs, cotangent, log_norms = scratch
    sums = jnp.sum(
        cotangent[...].astype(F32) * outputs[...].astype(F32), axis=0, keepdims=True
    )
    zh, x, y = lax.axis_index("zh"), lax.axis_index("x"), lax.axis_index("y")
    head = 4 * y + 2 * zh + x // 2
    mine = lax.broadcasted_iota(jnp.int32, (HEADS, ROWS), 0) == head
    norms = jnp.sum(jnp.where(mine, log_norms[...], 0.0), axis=0, keepdims=True)
    message[:PART, :] = queries[...]
    message[PART : 2 * PART, :] = cotangent[...]
    message[2 * PART :, :] = stat_rows(pieces(sums) + pieces(norms))


def make_message(*args):
    return call(
        message_kernel,
        shape(2 * PART + STAT, ROWS),
        [HBM] * 4,
        VMEM,
        4,
        "message",
        [pltpu.VMEM(a.shape, a.dtype) for a in args] + [pltpu.SemaphoreType.DMA((4,))],
    )(*map(in_hbm, args))


def bundle_kernel(own, other, out):
    odd = lax.rem(lax.axis_index("x"), 2)
    for ref, place in ((own, odd), (other, 1 - odd)):
        start = pl.multiple_of(place * PART, PART)
        out[pl.ds(start, PART), :] = ref[:PART, :]
        out[pl.ds(start + 2 * PART, PART), :] = ref[PART : 2 * PART, :]
    one, two = own[2 * PART :, :].astype(F32), other[2 * PART :, :].astype(F32)
    both = one + two
    rows = pieces(both[0:1] + both[1:2] + both[2:3])
    out[4 * PART :, :] = stat_rows(rows + [one[3:6]])


def bundle(*args):
    return call(
        bundle_kernel, shape(4 * PART + STAT, ROWS), [VMEM] * 2, VMEM, 4, "bundle"
    )(*args)


def slot_columns(s):
    y, x = peer(s, lax.axis_index("core"))
    zh = (lax.axis_index("zh") + x) % 2
    return pl.ds(pl.multiple_of((4 * y + 2 * zh + x // 2) * DH, DH), DH)


def split_kernel(keys, values, out, held, in_sem, out_sem):
    pieces = [(s, a) for s in range(16) for a in range(2)]
    reads, writes = [], []
    for s, a in pieces:
        array = (keys, values)[a]
        at = held.at[s, a]
        number = 2 * s + a
        reads.append(
            pltpu.make_async_copy(array.at[:, slot_columns(s)], at, in_sem.at[number])
        )
        writes.append(pltpu.make_async_copy(at, out.at[s, a], out_sem.at[number]))
    for copy in reads:
        copy.start()
    for read, write in zip(reads, writes):
        read.wait()
        write.start()
    for copy in writes:
        copy.wait()


def split(keys, values):
    return call(
        split_kernel,
        pltpu.HBM((16, 2, KEYS, DH), BF16),
        [HBM] * 2,
        HBM,
        8,
        "split",
        [
            pltpu.VMEM((16, 2, KEYS, DH), BF16),
            pltpu.SemaphoreType.DMA((32,)),
            pltpu.SemaphoreType.DMA((32,)),
        ],
        pl.CostEstimate(flops=0, bytes_accessed=8 * MIB, transcendentals=0),
    )(in_hbm(keys), in_hbm(values))


def join_kernel(chunks, own, other, keys, values, queries):
    queries[...] = (own[...].astype(F32) + other[...].astype(F32)).astype(BF16)
    for s in range(16):
        columns = slot_columns(s)
        keys[:, columns] = chunks[s, 0]
        values[:, columns] = chunks[s, 1]


def join(chunks, own, other):
    out = shape(KEYS, HEADS * DH)
    outs = [out, out, shape(PART, ROWS)]
    return call(join_kernel, outs, [VMEM] * 3, [VMEM] * 3, 8, "join")(
        chunks, own, other
    )


def dot(a, b, ca, cb):
    return lax.dot_general(a, b, (((ca,), (cb,)), ((), ())), preferred_element_type=F32)


def assemble_kernel(*refs):
    mine, theirs, (qt, out, stat, dt, sem) = refs[:4], refs[4:8], refs[8:]
    core = lax.axis_index("core")
    for k in range(4):
        zl = k
        for ref, c in ((mine[k], core), (theirs[k], 1 - core)):
            for xl in range(2):
                to = pl.ds(pl.multiple_of((2 * xl + c) * PART, PART), PART)
                qt[zl, to, :] = ref[xl * PART : (xl + 1) * PART, :]
                dt[zl, to, :] = ref[(2 + xl) * PART : (3 + xl) * PART, :]
        one = mine[k][4 * PART :, :].astype(F32)
        both = one + theirs[k][4 * PART :, :].astype(F32)
        stat[zl, 0:1, :] = both[0:1] + both[1:2] + both[2:3]
        stat[zl, 1:2, :] = (one[3:4] + one[4:5] + one[5:6]) * LOG2E
    copy = pltpu.make_async_copy(dt, out, sem)
    copy.start()
    copy.wait()


def assemble(mine, theirs):
    block = (4, DH, ROWS)
    return call(
        assemble_kernel,
        [shape(*block), pltpu.HBM(block, BF16), shape(4, 8, ROWS, dtype=F32)],
        [VMEM] * 8,
        [VMEM, HBM, VMEM],
        8,
        "assemble",
        [pltpu.VMEM(block, BF16), pltpu.SemaphoreType.DMA],
    )(*mine, *theirs)


def attention_kernel(
    qt, cotangent, stat, kv, grads, own, other, dt, dkv, dq, ds, sem, in_sem
):
    core = lax.axis_index("core")
    read = pltpu.make_async_copy(cotangent, dt, in_sem)
    read.start()
    read.wait()
    writes = []
    for block in range(4):
        rows = slice(block * 4 * KEYS, (block + 1) * 4 * KEYS)
        keys = kv[4 * block : 4 * block + 4, 0].reshape(4 * KEYS, DH)
        values = kv[4 * block : 4 * block + 4, 1].reshape(4 * KEYS, DH)
        weights, slopes = [], []
        for zl in range(4):
            score = dot(keys, qt[zl], 1, 0)
            weight = jnp.exp2(score * (FACTOR * LOG2E) - stat[zl, 1:2, :])
            slope = dot(values, dt[zl], 1, 0)
            grad = (weight * (slope - stat[zl, 0:1, :])).astype(BF16)
            weights.append(weight.astype(BF16))
            slopes.append(grad)
            ds[rows, zl * ROWS : (zl + 1) * ROWS] = grad
        value_grad = sum(dot(weights[zl], dt[zl], 1, 1) for zl in range(4))
        key_grad = sum(dot(slopes[zl], qt[zl], 1, 1) for zl in range(4)) * FACTOR
        for place in range(4):
            part = slice(place * KEYS, (place + 1) * KEYS)
            dkv[4 * block + place, 0] = key_grad[part].astype(BF16)
            dkv[4 * block + place, 1] = value_grad[part].astype(BF16)
        slots = slice(4 * block, 4 * block + 4)
        copy = pltpu.make_async_copy(dkv.at[slots], grads.at[slots], sem.at[block])
        copy.start()
        writes.append(copy)
    keys = kv[:, 0].reshape(16 * KEYS, DH)
    dq[...] = dot(keys, ds[...], 0, 0) * FACTOR
    for k in range(4):
        zl = k
        for xl in range(2):
            at = pl.ds(pl.multiple_of((2 * xl + core) * PART, PART), PART)
            own[k, xl] = dq[at, zl * ROWS : (zl + 1) * ROWS]
            at = pl.ds(pl.multiple_of((2 * xl + 1 - core) * PART, PART), PART)
            other[k, xl] = dq[at, zl * ROWS : (zl + 1) * ROWS].astype(BF16)
    for copy in writes:
        copy.wait()


def attention(qt, dt, stat, kv):
    part = (4, 2, PART, ROWS)
    return call(
        attention_kernel,
        [pltpu.HBM((16, 2, KEYS, DH), BF16), shape(*part, dtype=F32), shape(*part)],
        [VMEM, HBM, VMEM, VMEM],
        [HBM, VMEM, VMEM],
        32,
        "attention",
        [
            pltpu.VMEM((4, DH, ROWS), BF16),
            pltpu.VMEM((16, 2, KEYS, DH), BF16),
            pltpu.VMEM((DH, 4 * ROWS), F32),
            pltpu.VMEM((16 * KEYS, 4 * ROWS), BF16),
            pltpu.SemaphoreType.DMA((8,)),
            pltpu.SemaphoreType.DMA,
        ],
        pl.CostEstimate(
            flops=5 * 2 * 2048 * 1024 * 256,
            bytes_accessed=8 * MIB,
            transcendentals=2048 * 1024,
        ),
    )(qt, in_hbm(dt), stat, kv)


def core_sum_kernel(own, other, *outs):
    for d, out in enumerate(outs):
        out[...] = (own[d] + other[d].astype(F32)).astype(BF16)


def core_sum(own, other):
    return call(
        core_sum_kernel,
        [shape(2, PART, ROWS)] * 4,
        [VMEM] * 2,
        [VMEM] * 4,
        4,
        "core_sum",
    )(own, other)


def line_sum_kernel(*refs):
    total = refs[0][...].astype(F32)
    for part in refs[1:4]:
        total = total + part[...].astype(F32)
    refs[4][...] = total.astype(BF16)


def line_sum(parts):
    out = shape(2, PART, ROWS)
    return call(line_sum_kernel, out, [VMEM] * 4, VMEM, 4, "line_sum")(*parts)


def pick_kernel(kept, crossed, own, other):
    odd = lax.rem(lax.axis_index("x"), 2)

    @pl.when(odd == 0)
    def _():
        own[...] = kept[0]
        other[...] = kept[1]

    @pl.when(odd == 1)
    def _():
        own[...] = crossed[1]
        other[...] = crossed[0]


def pick(kept, crossed):
    outs = [shape(PART, ROWS)] * 2
    return call(pick_kernel, outs, [VMEM] * 2, [VMEM] * 2, 4, "pick")(kept, crossed)


def choose_kernel(kept, crossed, out):
    odd = lax.rem(lax.axis_index("x"), 2)

    @pl.when(odd == 0)
    def _():
        out[...] = kept[...]

    @pl.when(odd == 1)
    def _():
        out[...] = crossed[...]


def choose(kept, crossed):
    out = shape(*kept.shape)
    return call(choose_kernel, out, [VMEM] * 2, VMEM, 4, "choose")(kept, crossed)


def local(queries, outputs, cotangent, log_norms, memory_keys, memory_values):
    message = make_message(queries.T, outputs.T, cotangent.T, log_norms.T)
    other = lax.ppermute(message, "x", NEXT)
    chunks = split(memory_keys, memory_values)
    chunks, other = lax.optimization_barrier((chunks, other))
    received = exchange(chunks)
    part = bundle(message, other)
    part = choose(part, lax.ppermute(part, LINE, MIRROR))
    mine = [part] + [lax.ppermute(part, "zl", turn(k)) for k in (1, 2, 3)]
    theirs = [lax.ppermute(part, "core", SWAP) for part in mine]
    grads, own, other = attention(*assemble(mine, theirs), received)
    returned = exchange(grads)
    sums = core_sum(own, lax.ppermute(other, "core", SWAP))
    sums = [sums[0]] + [lax.ppermute(sums[k], "zl", turn(k)) for k in (1, 2, 3)]
    total = line_sum(sums)
    own, other = pick(total, lax.ppermute(total, LINE, MIRROR))
    other = lax.ppermute(other, "x", NEXT)
    key_grads, value_grads, query_grads = join(returned, own, other)
    return query_grads.T, key_grads, value_grads


def solution(mesh):
    fine = Mesh(mesh.devices.reshape(SIZES), AXES)
    return jax.shard_map(
        local,
        mesh=fine,
        in_specs=(
            P("zl", MEM),
            P("zl", MEM),
            P("zl", MEM),
            P("zl", None),
            P(MEM + ("zl",), None),
            P(MEM + ("zl",), None),
        ),
        out_specs=(P("zl", MEM), P(MEM + ("zl",), None), P(MEM + ("zl",), None)),
        check_vma=False,
    )
```

```python
import jax
import jax.numpy as jnp
from jax import lax
from jax.experimental import pallas as pl
from jax.experimental.pallas import tpu as pltpu
from jax.sharding import Mesh, PartitionSpec as P

AXES = ("y", "zh", "x", "core", "zl")
SIZES = (4, 2, 4, 2, 4)
MEM = ("y", "zh", "x", "core")
HEADS = 16
DH = 256
ROWS = 256
PART = 64
KEYS = 128
STAT = 16
FACTOR = DH**-0.5
LOG2E = 1.4426950408889634
MIB = 1024 * 1024
BF16, F32 = jnp.bfloat16, jnp.float32
HBM = pl.BlockSpec(memory_space=pltpu.HBM)
VMEM = pl.BlockSpec(memory_space=pltpu.VMEM)


def call(kernel, outs, ins, out_specs, limit, name, scratch=(), cost=None):
    return pl.pallas_call(
        kernel,
        out_shape=outs,
        in_specs=ins,
        out_specs=out_specs,
        scratch_shapes=list(scratch),
        compiler_params=pltpu.CompilerParams(vmem_limit_bytes=limit * MIB),
        cost_estimate=cost,
        name=name,
    )


def shape(*dims, dtype=BF16):
    return jax.ShapeDtypeStruct(dims, dtype)


LINE = ("zh", "x", "zl")
MIRROR = [
    ((zh * 4 + x) * 4 + zl, ((1 - zh) * 4 + x) * 4 + 3 - zl)
    for zh in range(2)
    for x in (1, 3)
    for zl in range(4)
]


def turn(k):
    return [(i, i ^ k) for i in range(4)]


NEXT = [(0, 1), (1, 0), (2, 3), (3, 2)]
SWAP = [(0, 1), (1, 0)]


def peer(slot, core):
    return (slot // 4 + 2 * core) % 4, (slot + 2 * core) % 4


def exchange(chunks):
    groups = []
    for zh in range(2):
        for core in range(2):
            for zl in range(4):
                peers = [peer(slot, core) for slot in range(16)]
                groups.append(
                    [(((y * 2 + zh) * 4 + x) * 2 + core) * 4 + zl for y, x in peers]
                )
    return lax.all_to_all(
        chunks, AXES, split_axis=0, concat_axis=0, tiled=True, axis_index_groups=groups
    )


def pieces(value):
    high = value.astype(BF16)
    rest = value - high.astype(F32)
    middle = rest.astype(BF16)
    low = (rest - middle.astype(F32)).astype(BF16)
    return [high.astype(F32), middle.astype(F32), low.astype(F32)]


def in_hbm(array):
    return pltpu.with_memory_space_constraint(array, pltpu.HBM)


def stat_rows(rows):
    pad = jnp.zeros((STAT - 6, ROWS), F32)
    return jnp.concatenate(rows + [pad], axis=0).astype(BF16)


def message_kernel(*refs):
    message, scratch, sem = refs[4], refs[5:9], refs[9]
    copies = [
        pltpu.make_async_copy(refs[i], scratch[i], sem.at[i]) for i in range(4)
    ]
    for copy in copies:
        copy.start()
    for copy in copies:
        copy.wait()
    queries, outputs, cotangent, log_norms = scratch
    sums = jnp.sum(
        cotangent[...].astype(F32) * outputs[...].astype(F32), axis=0, keepdims=True
    )
    zh, x, y = lax.axis_index("zh"), lax.axis_index("x"), lax.axis_index("y")
    head = 4 * y + 2 * zh + x // 2
    mine = lax.broadcasted_iota(jnp.int32, (HEADS, ROWS), 0) == head
    norms = jnp.sum(jnp.where(mine, log_norms[...], 0.0), axis=0, keepdims=True)
    message[:PART, :] = queries[...]
    message[PART : 2 * PART, :] = cotangent[...]
    message[2 * PART :, :] = stat_rows(pieces(sums) + pieces(norms))


def make_message(*args):
    return call(
        message_kernel,
        shape(2 * PART + STAT, ROWS),
        [HBM] * 4,
        VMEM,
        4,
        "message",
        [pltpu.VMEM(a.shape, a.dtype) for a in args] + [pltpu.SemaphoreType.DMA((4,))],
    )(*map(in_hbm, args))


def bundle_kernel(own, other, out):
    odd = lax.rem(lax.axis_index("x"), 2)
    for ref, place in ((own, odd), (other, 1 - odd)):
        start = pl.multiple_of(place * PART, PART)
        out[pl.ds(start, PART), :] = ref[:PART, :]
        out[pl.ds(start + 2 * PART, PART), :] = ref[PART : 2 * PART, :]
    one, two = own[2 * PART :, :].astype(F32), other[2 * PART :, :].astype(F32)
    both = one + two
    rows = pieces(both[0:1] + both[1:2] + both[2:3])
    out[4 * PART :, :] = stat_rows(rows + [one[3:6]])


def bundle(*args):
    return call(
        bundle_kernel, shape(4 * PART + STAT, ROWS), [VMEM] * 2, VMEM, 4, "bundle"
    )(*args)


def slot_columns(s):
    y, x = peer(s, lax.axis_index("core"))
    zh = (lax.axis_index("zh") + x) % 2
    return pl.ds(pl.multiple_of((4 * y + 2 * zh + x // 2) * DH, DH), DH)


def split_kernel(keys, values, out, held, in_sem, out_sem):
    pieces = [(s, a) for s in range(16) for a in range(2)]
    reads, writes = [], []
    for s, a in pieces:
        array = (keys, values)[a]
        at = held.at[s, a]
        number = 2 * s + a
        reads.append(
            pltpu.make_async_copy(array.at[:, slot_columns(s)], at, in_sem.at[number])
        )
        writes.append(pltpu.make_async_copy(at, out.at[s, a], out_sem.at[number]))
    for copy in reads:
        copy.start()
    for read, write in zip(reads, writes):
        read.wait()
        write.start()
    for copy in writes:
        copy.wait()


def split(keys, values):
    return call(
        split_kernel,
        pltpu.HBM((16, 2, KEYS, DH), BF16),
        [HBM] * 2,
        HBM,
        8,
        "split",
        [
            pltpu.VMEM((16, 2, KEYS, DH), BF16),
            pltpu.SemaphoreType.DMA((32,)),
            pltpu.SemaphoreType.DMA((32,)),
        ],
        pl.CostEstimate(flops=0, bytes_accessed=8 * MIB, transcendentals=0),
    )(in_hbm(keys), in_hbm(values))


def join_kernel(chunks, own, other, keys, values, queries):
    queries[...] = (own[...].astype(F32) + other[...].astype(F32)).astype(BF16)
    for s in range(16):
        columns = slot_columns(s)
        keys[:, columns] = chunks[s, 0]
        values[:, columns] = chunks[s, 1]


def join(chunks, own, other):
    out = shape(KEYS, HEADS * DH)
    outs = [out, out, shape(PART, ROWS)]
    return call(join_kernel, outs, [VMEM] * 3, [VMEM] * 3, 8, "join")(
        chunks, own, other
    )


def dot(a, b, ca, cb):
    return lax.dot_general(a, b, (((ca,), (cb,)), ((), ())), preferred_element_type=F32)


def assemble_kernel(*refs):
    mine, theirs, (qt, out, stat, dt, sem) = refs[:4], refs[4:8], refs[8:]
    core = lax.axis_index("core")
    for k in range(4):
        zl = k
        for ref, c in ((mine[k], core), (theirs[k], 1 - core)):
            for xl in range(2):
                to = pl.ds(pl.multiple_of((2 * xl + c) * PART, PART), PART)
                qt[zl, to, :] = ref[xl * PART : (xl + 1) * PART, :]
                dt[zl, to, :] = ref[(2 + xl) * PART : (3 + xl) * PART, :]
        one = mine[k][4 * PART :, :].astype(F32)
        both = one + theirs[k][4 * PART :, :].astype(F32)
        stat[zl, 0:1, :] = both[0:1] + both[1:2] + both[2:3]
        stat[zl, 1:2, :] = (one[3:4] + one[4:5] + one[5:6]) * LOG2E
    copy = pltpu.make_async_copy(dt, out, sem)
    copy.start()
    copy.wait()


def assemble(mine, theirs):
    block = (4, DH, ROWS)
    return call(
        assemble_kernel,
        [shape(*block), pltpu.HBM(block, BF16), shape(4, 8, ROWS, dtype=F32)],
        [VMEM] * 8,
        [VMEM, HBM, VMEM],
        8,
        "assemble",
        [pltpu.VMEM(block, BF16), pltpu.SemaphoreType.DMA],
    )(*mine, *theirs)


def attention_kernel(
    qt, cotangent, stat, kv, grads, own, other, dt, dkv, dq, ds, sem, in_sem
):
    core = lax.axis_index("core")
    read = pltpu.make_async_copy(cotangent, dt, in_sem)
    read.start()
    read.wait()
    writes = []
    for block in range(2):
        rows = slice(block * 8 * KEYS, (block + 1) * 8 * KEYS)
        keys = kv[8 * block : 8 * block + 8, 0].reshape(8 * KEYS, DH)
        values = kv[8 * block : 8 * block + 8, 1].reshape(8 * KEYS, DH)
        weights, slopes = [], []
        for zl in range(4):
            score = dot(keys, qt[zl], 1, 0)
            weight = jnp.exp2(score * (FACTOR * LOG2E) - stat[zl, 1:2, :])
            slope = dot(values, dt[zl], 1, 0)
            grad = (weight * (slope - stat[zl, 0:1, :])).astype(BF16)
            weights.append(weight.astype(BF16))
            slopes.append(grad)
            ds[rows, zl * ROWS : (zl + 1) * ROWS] = grad
        value_grad = sum(dot(weights[zl], dt[zl], 1, 1) for zl in range(4))
        key_grad = sum(dot(slopes[zl], qt[zl], 1, 1) for zl in range(4)) * FACTOR
        for place in range(8):
            part = slice(place * KEYS, (place + 1) * KEYS)
            dkv[8 * block + place, 0] = key_grad[part].astype(BF16)
            dkv[8 * block + place, 1] = value_grad[part].astype(BF16)
        slots = slice(8 * block, 8 * block + 8)
        copy = pltpu.make_async_copy(dkv.at[slots], grads.at[slots], sem.at[block])
        copy.start()
        writes.append(copy)
    keys = kv[:, 0].reshape(16 * KEYS, DH)
    dq[...] = dot(keys, ds[...], 0, 0) * FACTOR
    for k in range(4):
        zl = k
        for xl in range(2):
            at = pl.ds(pl.multiple_of((2 * xl + core) * PART, PART), PART)
            own[k, xl] = dq[at, zl * ROWS : (zl + 1) * ROWS]
            at = pl.ds(pl.multiple_of((2 * xl + 1 - core) * PART, PART), PART)
            other[k, xl] = dq[at, zl * ROWS : (zl + 1) * ROWS].astype(BF16)
    for copy in writes:
        copy.wait()


def attention(qt, dt, stat, kv):
    part = (4, 2, PART, ROWS)
    return call(
        attention_kernel,
        [pltpu.HBM((16, 2, KEYS, DH), BF16), shape(*part, dtype=F32), shape(*part)],
        [VMEM, HBM, VMEM, VMEM],
        [HBM, VMEM, VMEM],
        32,
        "attention",
        [
            pltpu.VMEM((4, DH, ROWS), BF16),
            pltpu.VMEM((16, 2, KEYS, DH), BF16),
            pltpu.VMEM((DH, 4 * ROWS), F32),
            pltpu.VMEM((16 * KEYS, 4 * ROWS), BF16),
            pltpu.SemaphoreType.DMA((8,)),
            pltpu.SemaphoreType.DMA,
        ],
        pl.CostEstimate(
            flops=5 * 2 * 2048 * 1024 * 256,
            bytes_accessed=8 * MIB,
            transcendentals=2048 * 1024,
        ),
    )(qt, in_hbm(dt), stat, kv)


def core_sum_kernel(own, other, *outs):
    for d, out in enumerate(outs):
        out[...] = (own[d] + other[d].astype(F32)).astype(BF16)


def core_sum(own, other):
    return call(
        core_sum_kernel,
        [shape(2, PART, ROWS)] * 4,
        [VMEM] * 2,
        [VMEM] * 4,
        4,
        "core_sum",
    )(own, other)


def line_sum_kernel(*refs):
    total = refs[0][...].astype(F32)
    for part in refs[1:4]:
        total = total + part[...].astype(F32)
    refs[4][...] = total.astype(BF16)


def line_sum(parts):
    out = shape(2, PART, ROWS)
    return call(line_sum_kernel, out, [VMEM] * 4, VMEM, 4, "line_sum")(*parts)


def pick_kernel(kept, crossed, own, other):
    odd = lax.rem(lax.axis_index("x"), 2)

    @pl.when(odd == 0)
    def _():
        own[...] = kept[0]
        other[...] = kept[1]

    @pl.when(odd == 1)
    def _():
        own[...] = crossed[1]
        other[...] = crossed[0]


def pick(kept, crossed):
    outs = [shape(PART, ROWS)] * 2
    return call(pick_kernel, outs, [VMEM] * 2, [VMEM] * 2, 4, "pick")(kept, crossed)


def choose_kernel(kept, crossed, out):
    odd = lax.rem(lax.axis_index("x"), 2)

    @pl.when(odd == 0)
    def _():
        out[...] = kept[...]

    @pl.when(odd == 1)
    def _():
        out[...] = crossed[...]


def choose(kept, crossed):
    out = shape(*kept.shape)
    return call(choose_kernel, out, [VMEM] * 2, VMEM, 4, "choose")(kept, crossed)


def local(queries, outputs, cotangent, log_norms, memory_keys, memory_values):
    message = make_message(queries.T, outputs.T, cotangent.T, log_norms.T)
    other = lax.ppermute(message, "x", NEXT)
    chunks = split(memory_keys, memory_values)
    chunks, other = lax.optimization_barrier((chunks, other))
    received = exchange(chunks)
    part = bundle(message, other)
    part = choose(part, lax.ppermute(part, LINE, MIRROR))
    mine = [part] + [lax.ppermute(part, "zl", turn(k)) for k in (1, 2, 3)]
    theirs = [lax.ppermute(part, "core", SWAP) for part in mine]
    grads, own, other = attention(*assemble(mine, theirs), received)
    returned = exchange(grads)
    sums = core_sum(own, lax.ppermute(other, "core", SWAP))
    sums = [sums[0]] + [lax.ppermute(sums[k], "zl", turn(k)) for k in (1, 2, 3)]
    total = line_sum(sums)
    own, other = pick(total, lax.ppermute(total, LINE, MIRROR))
    other = lax.ppermute(other, "x", NEXT)
    key_grads, value_grads, query_grads = join(returned, own, other)
    return query_grads.T, key_grads, value_grads


def solution(mesh):
    fine = Mesh(mesh.devices.reshape(SIZES), AXES)
    return jax.shard_map(
        local,
        mesh=fine,
        in_specs=(
            P("zl", MEM),
            P("zl", MEM),
            P("zl", MEM),
            P("zl", None),
            P(MEM + ("zl",), None),
            P(MEM + ("zl",), None),
        ),
        out_specs=(P("zl", MEM), P(MEM + ("zl",), None), P(MEM + ("zl",), None)),
        check_vma=False,
    )
```
